512 devices in a mesh: ctx: 32 (over x_hi, y, core), ch: 16 (over x_lo, z).
Axes of the slice: x: 4 (x_hi: 2, x_lo: 2; x = x_hi * 2 + x_lo), y: 8, z: 8, core: 2. Of those that a mesh axis runs over, the one named last changes fastest.
Arguments:
- signal: bfloat16 [65536, 2048], P('ctx', 'ch'), may hold values from -6 to 6
- cond_in: bfloat16 [2048, 64], P('ch'), may hold values from -0.125 to 0.125
- cond_bias: float32 [64], replicated, may hold values from -4 to 4
- cond_out: bfloat16 [64, 2048], P(None, 'ch'), may hold values from -0.75 to 0.75
- skip_gain: float32 [2048], P('ch'), may hold values from 0.5 to 1.5
Outputs:
- mixed: bfloat16 [65536, 2048], P('ctx', 'ch')
The draws below stay inside these ranges and needn't reach their ends.
All inputs are finite; a program needn't handle non-finite values.
Results may differ from the reference program's by a relative error of at most 0.00125.
Values may be sent and summed in bfloat16 or wider, within the bound.
No kernel may reach another device: no remote copies, remote signals or barrier semaphores. Data moves between devices by JAX's collectives and lax.ppermute only.
A program may use at most 64 MiB of HBM per device.

```python
import jax
import jax.numpy as jnp
from jax import lax

D = 2048
HID = 64
SEQ = 65536


def level_of(own_key, shape, cuts, low, top_value):
    factor_of = 1.0
    for position, blocks in cuts:
        heights = jax.random.uniform(jax.random.fold_in(jax.random.fold_in(own_key, 6), position), (blocks,), jnp.float32, low / len(cuts), top_value / len(cuts))
        factor_of = factor_of * jnp.repeat(jnp.exp(heights), shape[position] // blocks).reshape((-1,) + (1,) * (len(shape) - 1 - position))
    return factor_of


def gaussian(stream_key, extent, scale, most, shards=(), held_as=jnp.bfloat16):
    values = scale * jax.random.normal(stream_key, extent, jnp.float32)
    if shards:
        values = values * level_of(stream_key, extent, shards, -0.22, 0.18)
    return jnp.clip(values, -most, most).astype(held_as)


def setup_inputs(seed: int = 0) -> dict:
    keys = jax.random.split(jax.random.key(seed), 6)
    return {
        "signal": gaussian(keys[0], (SEQ, D), 1.0, 6.0, ((0, 32), (1, 16))),
        "cond_in": gaussian(keys[1], (D, HID), D ** -0.5, 0.125, ((0, 16),)),
        "cond_bias": gaussian(keys[2], (HID,), 1.0, 4.0, (), jnp.float32),
        "cond_out": gaussian(keys[3], (HID, D), HID ** -0.5, 0.75, ((1, 16),)),
        "skip_gain": jnp.clip(1.0 + 0.1 * jax.random.normal(keys[4], (D,), jnp.float32), 0.5, 1.5),
    }


def reference(signal, cond_in, cond_bias, cond_out, skip_gain):
    seq_total, width = signal.shape
    block_width = min(width, 128)
    block_count = width // block_width
    sig_blocks = signal.reshape(seq_total, block_count, block_width).transpose(1, 0, 2)
    in_blocks = cond_in.reshape(block_count, block_width, HID)
    out_blocks = cond_out.reshape(HID, block_count, block_width).transpose(1, 0, 2)
    gain_blocks = skip_gain.reshape(block_count, block_width)

    def spectrum_of(block):
        return jnp.fft.fft(block.astype(jnp.float32), axis=0)

    def accumulate(total, pieces):
        block, weights = pieces
        spectrum = spectrum_of(block)
        power = spectrum.real * spectrum.real + spectrum.imag * spectrum.imag
        feature = jnp.log1p(power / seq_total)
        term = jnp.dot(feature, weights.astype(jnp.float32), precision=lax.Precision.HIGHEST)
        return total + term, None

    start_total = jnp.zeros((seq_total, HID), jnp.float32)
    pre, _ = lax.scan(accumulate, start_total, (sig_blocks, in_blocks))
    hidden = jax.nn.gelu(pre + cond_bias.astype(jnp.float32), approximate=False)

    def produce(pieces):
        block, weights, gains = pieces
        spectrum = spectrum_of(block)
        spectral_gain = jnp.dot(hidden, weights.astype(jnp.float32), precision=lax.Precision.HIGHEST)
        response = jnp.fft.ifft(spectrum * spectral_gain, axis=0).real
        combined = response + gains.astype(jnp.float32)[None, :] * block.astype(jnp.float32)
        return combined.astype(jnp.bfloat16)

    mixed_blocks = lax.map(produce, (sig_blocks, out_blocks, gain_blocks))
    return mixed_blocks.transpose(1, 0, 2).reshape(seq_total, width)
```

```python
import functools
import math

import jax
import jax.numpy as jnp
import numpy as np
from jax import lax
from jax.experimental import pallas as pl
from jax.experimental.pallas import tpu as pltpu
from jax.sharding import PartitionSpec as P

f32, bf16, f16 = jnp.float32, jnp.bfloat16, jnp.float16

RADIX = 256
HALF = RADIX // 2
SEQ = RADIX * RADIX
GAIN_SCALE = 0.25


def split_const(values):
    high = values.astype(np.float32).astype(jnp.bfloat16)
    low = (values - high.astype(np.float64)).astype(np.float32).astype(jnp.bfloat16)
    return high, low


@functools.lru_cache(maxsize=None)
def tables():
    n = np.arange(RADIX, dtype=np.float64)
    k = np.arange(HALF, dtype=np.float64)
    tau = 2.0 * np.pi
    angle = tau * np.outer(k, n) / RADIX
    first = np.concatenate([np.cos(angle), -np.sin(angle)], 0)
    first[HALF] = np.cos(math.pi * n)
    first = np.concatenate(split_const(first), 0)
    angle = tau * np.outer(k, n) / SEQ
    cos_f, sin_f = np.cos(angle), np.sin(angle)
    cos_g = cos_f.copy()
    cos_g[0] = 0.0
    shared = tau * n * (HALF + SEQ // 2) / SEQ
    twf = np.stack([cos_f, sin_f, cos_g]).astype(np.float32)
    row0 = np.zeros((3, 8, RADIX))
    row0[0, 0], row0[1, 0] = np.cos(shared), np.sin(shared)
    row0[2, :] = np.cos(math.pi * n)
    row0 = row0.astype(np.float32)
    angle = tau * np.outer(n, n) / RADIX
    wre, wim = np.cos(angle), -np.sin(angle)
    full = [np.concatenate([wre, -wim], 1), np.concatenate([wim, wre], 1)]
    second = np.stack([np.concatenate([f[:HALF] for f in full], 0),
                       np.concatenate([f[HALF:] for f in full], 0)])
    second = np.stack(split_const(second))
    vre, vim = np.cos(angle), np.sin(angle)
    inv = np.stack([
        np.concatenate([np.concatenate([vre[:, s], -vim[:, s]], 1),
                        np.concatenate([vim[:, s], vre[:, s]], 1)], 0)
        for s in (slice(0, HALF), slice(HALF, RADIX))])
    inv = np.stack(split_const(inv))
    angle = tau * np.outer(n, k) / SEQ
    twi = np.stack([np.cos(angle), np.sin(angle),
                    np.repeat(np.cos(shared)[:, None], HALF, 1),
                    np.repeat(np.sin(shared)[:, None], HALF, 1)]).astype(np.float32)
    angle = tau * np.outer(n, k) / RADIX
    last = np.concatenate([np.cos(angle), -np.sin(angle)], 1)
    last[:, HALF] = np.cos(math.pi * n)
    last = np.stack(split_const(last * (2.0 / SEQ)))
    return dict(first=first, twf=twf, row0=row0, second=second, inv=inv, twi=twi, last=last)


def split(x):
    high = x.astype(bf16)
    return high, (x - high.astype(f32)).astype(bf16)


def mm(a, b):
    return jnp.dot(a, b, preferred_element_type=f32)


def nt(a, b):
    return lax.dot_general(a, b, (((1,), (1,)), ((), ())), preferred_element_type=f32)


def iota(shape, axis):
    return lax.broadcasted_iota(jnp.int32, shape, axis)


def pack_kernel(x_ref, out_ref, left, right):
    rows = x_ref.shape[0] // RADIX
    chan = x_ref.shape[1]
    for a in range(rows):
        block = x_ref[RADIX * a : RADIX * (a + 1), :].astype(f32).T
        left[pl.ds(a, chan, stride=rows), :] = block[:, :128]
        right[pl.ds(a, chan, stride=rows), :] = block[:, 128:]
    out_ref[:, :, :128] = left[...].astype(bf16).reshape(out_ref.shape[:2] + (128,))
    out_ref[:, :, 128:] = right[...].astype(bf16).reshape(out_ref.shape[:2] + (128,))


def unpack_kernel(r_ref, out_ref, left, right):
    rows = out_ref.shape[0] // RADIX
    chan = out_ref.shape[1]
    left[...] = r_ref[:, :, :128].astype(f32).reshape(left.shape)
    right[...] = r_ref[:, :, 128:].astype(f32).reshape(right.shape)
    for a in range(rows):
        out_ref[RADIX * a : RADIX * a + 128, :] = (
            left[pl.ds(a, chan, stride=rows), :].T.astype(bf16))
        out_ref[RADIX * a + 128 : RADIX * (a + 1), :] = (
            right[pl.ds(a, chan, stride=rows), :].T.astype(bf16))


def weights_kernel(members, per, rows, cin_ref, cout_ref, win_ref, wout_ref):
    chan, hid = cin_ref.shape
    big = per * members * rows
    lane = iota((chan, big), 1)
    pick = per * ((lane // rows) % members) + lane // (members * rows)
    rep = (iota((chan, big), 0) == pick).astype(f32).astype(bf16)
    spread = lax.dot_general(cin_ref[...], rep, (((0,), (0,)), ((), ())),
                             preferred_element_type=f32)
    lane = iota((hid, big), 1) % rows
    for k in range(rows):
        win_ref[k * hid : (k + 1) * hid, :] = jnp.where(lane == k, spread, 0.0).astype(bf16)
    wide = rows * hid
    copy = (iota((hid, wide), 1) % hid == iota((hid, wide), 0)).astype(f32).astype(bf16)
    columns = mm(jnp.transpose(cout_ref[...].astype(f32)).astype(bf16), copy)
    spread = lax.dot_general(rep, columns.astype(bf16), (((0,), (0,)), ((), ())),
                             preferred_element_type=f32)
    keep = iota((big, wide), 0) % rows == iota((big, wide), 1) // hid
    wout_ref[...] = jnp.where(keep, spread, 0.0).astype(bf16)


def forward_kernel(per, rows, r_ref, first_ref, twf_ref, row0_ref, second_ref,
                   feat_ref, spec_ref, nyq_ref, hi, lo, hi2, lo2):
    members = r_ref.shape[0]
    values = r_ref[...].astype(f32)
    first_row = iota((8, RADIX), 0) == 0
    spare = jnp.zeros((8, 128), f32)
    feat_spare = jnp.zeros((8, 128), f32)
    spare_lane = iota((8, 128), 1)
    for c in range(per):
        x = values[:, rows * c : rows * (c + 1), :].reshape(RADIX, RADIX).astype(bf16)
        a = mm(first_ref[...], x)
        a = a[:RADIX] + a[RADIX:]
        re, im = a[:HALF], a[HALF:]
        out_re = re * twf_ref[0] + im * twf_ref[1]
        out_im = im * twf_ref[2] - re * twf_ref[1]
        place = pl.ds(HALF * c, HALF)
        for at, part in ((0, out_re), (RADIX, out_im)):
            high, low = split(part)
            hi[place, at : at + RADIX], lo[place, at : at + RADIX] = high, low
            hi2[place, at : at + RADIX], lo2[place, at : at + RADIX] = high, low
        lead = im[0:8]
        top = pl.ds(HALF * c, 16)
        alt_re = jnp.concatenate(
            [jnp.where(first_row, lead * row0_ref[0], out_re[0:8]), out_re[8:16]], 0)
        alt_im = jnp.concatenate(
            [jnp.where(first_row, -lead * row0_ref[1], out_im[0:8]), out_im[8:16]], 0)
        for at, part in ((0, alt_re), (RADIX, alt_im)):
            high, low = split(part)
            hi2[top, at : at + RADIX], lo2[top, at : at + RADIX] = high, low
        nyq = jnp.sum(re[0:1] * row0_ref[2, 0:1], axis=1, keepdims=True)
        spare = jnp.where(spare_lane == c, nyq, spare)
    feat_spare = jnp.log1p(spare * spare * (1.0 / SEQ))
    nyq_ref[...] = spare
    width = HALF * per
    feat_ref[:, :, width:] = jnp.broadcast_to(feat_spare[None], (members, rows, 128))
    for part, (h, l) in enumerate(((hi, lo), (hi2, lo2))):
        s = (nt(second_ref[0, part], h[...]) + nt(second_ref[0, part], l[...])
             + nt(second_ref[1, part], h[...]))
        spec_ref[part] = s
        re, im = s[:HALF], s[HALF:]
        feature = jnp.log1p((re * re + im * im) * (1.0 / SEQ))
        count = HALF // rows
        feat_ref[part * count : (part + 1) * count, :, :width] = feature.reshape(
            count, rows, width)


def reduce_kernel(per, rows, hid, f_ref, win_ref, out_ref):
    members = f_ref.shape[0]
    groups = out_ref.shape[0]
    chunk = members * rows
    f = f_ref[...].reshape(chunk, f_ref.shape[2])
    stack = jnp.concatenate([f[:, HALF * c : HALF * (c + 1)] for c in range(per)], 0)
    high, low = split(stack)
    pre = mm(win_ref[...], jnp.concatenate([high, low], 1))
    pre = pre[:, :HALF] + pre[:, HALF:]
    main = pre.shape[0] // groups
    out_ref[:, :main, :] = pre.reshape(groups, main, HALF)
    last = f[:, HALF * per :]
    lane = iota(last.shape, 1)
    stack = jnp.concatenate([jnp.where(lane == c, last, 0.0) for c in range(per)], 0)
    high, low = split(stack)
    extra = mm(win_ref[:hid], jnp.concatenate([high, low], 1))
    extra = jnp.sum(extra, axis=1, keepdims=True)
    extra = jnp.sum(jnp.where(iota((hid, 128), 0) == iota((hid, 128), 1), extra, 0.0),
                    axis=0, keepdims=True)
    out_ref[:, main:, :] = jnp.broadcast_to(extra[None], (groups, 8, 128))


def gelu(v):
    return 0.5 * v * (1.0 + lax.erf(v * math.sqrt(0.5)))


def hidden_kernel(main, hid, r_ref, bias_ref, cout_ref, out_ref, gain_ref):
    groups = r_ref.shape[0]
    total = r_ref[0]
    for g in range(1, groups):
        total = total + r_ref[g]
    start = (lax.axis_index("ch") * main) % hid
    bias = bias_ref[...]
    column = jnp.sum(
        jnp.where(iota((main, hid), 1) == (iota((main, hid), 0) + start) % hid, bias, 0.0),
        axis=1, keepdims=True)
    hidden = gelu(total[:main] + column)
    out_ref[...] = jnp.broadcast_to(hidden[None], out_ref.shape)
    spare = gelu(total[main:, :hid] + bias)
    high, low = split(spare)
    gain_ref[...] = mm(high, cout_ref[...]) + mm(low, cout_ref[...])


def gain_kernel(per, rows, h_ref, wout_ref, out_ref):
    hidden = h_ref[...].reshape(wout_ref.shape[1], HALF)
    high, low = split(hidden)
    g = mm(wout_ref[...], jnp.concatenate([high, low], 1))
    g = (g[:, :HALF] + g[:, HALF:]) * GAIN_SCALE
    chunk = g.shape[0] // per
    members = out_ref.shape[0]
    for c in range(per):
        out_ref[:, :, HALF * c : HALF * (c + 1)] = g[chunk * c : chunk * (c + 1)].reshape(
            members, rows, HALF)


def inverse_kernel(per, rows, g_ref, spec_ref, nyq_ref, gain_ref, skip_ref, r_ref,
                   inv_ref, twi_ref, last_ref, row0_ref, out_ref):
    members = g_ref.shape[0]
    width = HALF * per
    count = members // 2
    sums = []
    for part in range(2):
        g = g_ref[part * count : (part + 1) * count].reshape(HALF, width)
        g = g * (1.0 / GAIN_SCALE)
        if part == 0:
            dc = (iota((HALF, width), 0) == 0) & (iota((HALF, width), 1) % HALF == 0)
            g = jnp.where(dc, 0.5 * g, g)
        s = spec_ref[part]
        high, low = split(jnp.concatenate([s[:HALF] * g, s[HALF:] * g], 0))
        sums.append(mm(inv_ref[0, part], high) + mm(inv_ref[0, part], low)
                    + mm(inv_ref[1, part], high))
    own = lax.axis_index("ctx") * per
    lane = iota((1, 128), 1)
    lane0 = iota((RADIX, HALF), 1) == 0
    pieces = []
    for c in range(per):
        cols = slice(HALF * c, HALF * (c + 1))
        top_re, top_im = sums[0][:RADIX, cols], sums[0][RADIX:, cols]
        bot_re, bot_im = sums[1][:RADIX, cols], sums[1][RADIX:, cols]
        re = jnp.where(lane0, top_re, top_re + bot_re)
        im = top_im + bot_im
        out_re = jnp.where(lane0, re, re * twi_ref[0] - im * twi_ref[1])
        out_im = jnp.where(lane0, bot_re * twi_ref[2] - bot_im * twi_ref[3],
                           re * twi_ref[1] + im * twi_ref[0])
        high, low = split(jnp.concatenate([out_re, out_im], 1))
        y = nt(last_ref[0], high) + nt(last_ref[0], low) + nt(last_ref[1], high)
        mine = lane == own + c
        skip = jnp.sum(jnp.where(mine, skip_ref[...], 0.0), axis=1, keepdims=True)
        gain = jnp.sum(jnp.where(mine, gain_ref[0:1], 0.0), axis=1, keepdims=True)
        spare = jnp.sum(jnp.where(lane == c, nyq_ref[0:1], 0.0), axis=1, keepdims=True)
        x = r_ref[:, rows * c : rows * (c + 1), :].astype(f32).reshape(RADIX, RADIX)
        y = y + (spare * gain * (1.0 / SEQ)) * row0_ref[2, 0:1] + skip * x
        pieces.append(y.reshape(members, rows, RADIX))
    out_ref[...] = jnp.concatenate(pieces, 1).astype(bf16)


def call(kernel, outs, scratch=(), flops=0, interpret=False):
    vmem = pl.BlockSpec(memory_space=pltpu.VMEM)
    many = isinstance(outs, (list, tuple))

    def run(*args):
        return pl.pallas_call(
            kernel,
            out_shape=outs,
            in_specs=[vmem] * len(args),
            out_specs=[vmem] * len(outs) if many else vmem,
            scratch_shapes=list(scratch),
            compiler_params=pltpu.CompilerParams(vmem_limit_bytes=40 * 1024 * 1024),
        )(*args)

    return run


def exchange(x, axis):
    return lax.all_to_all(x, axis, split_axis=0, concat_axis=0, tiled=True)


def on_device(signal, cond_in, cond_bias, cond_out, skip_gain):
    shape = jax.ShapeDtypeStruct
    members = lax.axis_size("ctx")
    groups = lax.axis_size("ch")
    seq_local, chan = signal.shape
    hid = cond_in.shape[1]
    per = chan // members
    rows = seq_local // RADIX
    width = HALF * per
    t = {name: jnp.asarray(value) for name, value in tables().items()}
    halves = [pltpu.VMEM((chan * rows, 128), f32)] * 2
    piece = shape((members, per * rows, RADIX), bf16)

    packed = call(pack_kernel, piece, halves)(signal)
    received = exchange(packed, "ctx")
    big = per * members * rows
    win, wout = call(functools.partial(weights_kernel, members, per, rows),
                     [shape((rows * hid, big), bf16), shape((big, rows * hid), bf16)])(
                         cond_in, cond_out)
    feat, spec, nyq = call(
        functools.partial(forward_kernel, per, rows),
        [shape((members, rows, width + 128), f32), shape((2, RADIX, width), f32),
         shape((8, 128), f32)],
        [pltpu.VMEM((width, 2 * RADIX), bf16)] * 4)(
            received, t["first"], t["twf"], t["row0"], t["second"])
    feat = exchange(feat.astype(f16), "ctx").astype(f32)
    main = rows * hid // groups
    partial = call(functools.partial(reduce_kernel, per, rows, hid),
                   shape((groups, main + 8, HALF), f32))(feat, win)
    partial = exchange(partial, "ch")
    hidden, spare_gain = call(functools.partial(hidden_kernel, main, hid),
                              [shape((groups, main, HALF), f32), shape((8, chan), f32)])(
                                  partial, cond_bias.reshape(1, hid), cond_out)
    hidden = exchange(hidden, "ch")
    gain = call(functools.partial(gain_kernel, per, rows),
                shape((members, rows, width), f32))(hidden, wout)
    gain = exchange(gain.astype(f16), "ctx").astype(f32)
    mixed = call(functools.partial(inverse_kernel, per, rows), piece)(
        gain, spec, nyq, spare_gain, skip_gain.reshape(1, chan), received,
        t["inv"], t["twi"], t["last"], t["row0"])
    mixed = exchange(mixed, "ctx")
    return call(unpack_kernel, shape((seq_local, chan), bf16), halves)(mixed)


def solution(mesh):
    return jax.shard_map(
        on_device,
        mesh=mesh,
        in_specs=(P("ctx", "ch"), P("ch", None), P(), P(None, "ch"), P("ch")),
        out_specs=P("ctx", "ch"),
        check_vma=False,
    )
```

```python
import functools
import math

import jax
import jax.numpy as jnp
import numpy as np
from jax import lax
from jax.experimental import pallas as pl
from jax.experimental.pallas import tpu as pltpu
from jax.sharding import Mesh
from jax.sharding import PartitionSpec as P

f32, bf16, f16 = jnp.float32, jnp.bfloat16, jnp.float16

RADIX = 256
HALF = RADIX // 2
SEQ = RADIX * RADIX
GAIN_SCALE = 0.25
IN_SCALE = 2.0**18
OUT_SCALE = 2.0**16


def split_const(values):
    high = values.astype(np.float32).astype(jnp.bfloat16)
    low = (values - high.astype(np.float64)).astype(np.float32).astype(jnp.bfloat16)
    return high, low


@functools.lru_cache(maxsize=None)
def tables():
    n = np.arange(RADIX, dtype=np.float64)
    k = np.arange(HALF, dtype=np.float64)
    tau = 2.0 * np.pi
    angle = tau * np.outer(k, n) / RADIX
    first = np.concatenate([np.cos(angle), -np.sin(angle)], 0)
    first[HALF] = np.cos(math.pi * n)
    first = np.concatenate(split_const(first), 0)
    angle = tau * np.outer(k, n) / SEQ
    cos_f, sin_f = np.cos(angle), np.sin(angle)
    cos_g = cos_f.copy()
    cos_g[0] = 0.0
    shared = tau * n * (HALF + SEQ // 2) / SEQ
    twf = np.stack([cos_f, sin_f, cos_g]).astype(np.float32)
    row0 = np.zeros((3, 8, RADIX))
    row0[0, 0], row0[1, 0] = np.cos(shared), np.sin(shared)
    row0[2, :] = np.cos(math.pi * n)
    row0 = row0.astype(np.float32)
    angle = tau * np.outer(n, n) / RADIX
    wre, wim = np.cos(angle), -np.sin(angle)
    full = [np.concatenate([wre, -wim], 1), np.concatenate([wim, wre], 1)]
    second = np.stack([np.concatenate([f[:HALF] for f in full], 0),
                       np.concatenate([f[HALF:] for f in full], 0)])
    second = np.stack(split_const(second))
    vre, vim = np.cos(angle), np.sin(angle)
    inv = np.stack([
        np.concatenate([np.concatenate([vre[:, s], -vim[:, s]], 1),
                        np.concatenate([vim[:, s], vre[:, s]], 1)], 0)
        for s in (slice(0, HALF), slice(HALF, RADIX))])
    inv = np.stack(split_const(inv))
    angle = tau * np.outer(n, k) / RADIX
    last = np.concatenate([np.cos(angle), -np.sin(angle)], 1)
    last[:, HALF] = np.cos(math.pi * n)
    last = np.stack(split_const(last * (2.0 / SEQ)))
    return dict(first=first, twf=twf, row0=row0, second=second, inv=inv, last=last)


def split(x):
    high = x.astype(bf16)
    return high, (x - high.astype(f32)).astype(bf16)


def mm(a, b):
    return jnp.dot(a, b, preferred_element_type=f32)


def nt(a, b):
    return lax.dot_general(a, b, (((1,), (1,)), ((), ())), preferred_element_type=f32)


def iota(shape, axis):
    return lax.broadcasted_iota(jnp.int32, shape, axis)


def pack_kernel(x_ref, out_ref, left, right):
    rows = x_ref.shape[0] // RADIX
    chan = x_ref.shape[1]
    for a in range(rows):
        block = x_ref[RADIX * a : RADIX * (a + 1), :].astype(f32).T
        left[pl.ds(a, chan, stride=rows), :] = block[:, :128]
        right[pl.ds(a, chan, stride=rows), :] = block[:, 128:]
    out_ref[:, :, :128] = left[...].astype(bf16).reshape(out_ref.shape[:2] + (128,))
    out_ref[:, :, 128:] = right[...].astype(bf16).reshape(out_ref.shape[:2] + (128,))


def unpack_kernel(r_ref, out_ref, left, right):
    rows = out_ref.shape[0] // RADIX
    chan = out_ref.shape[1]
    left[...] = r_ref[:, :, :128].astype(f32).reshape(left.shape)
    right[...] = r_ref[:, :, 128:].astype(f32).reshape(right.shape)
    for a in range(rows):
        out_ref[RADIX * a : RADIX * a + 128, :] = (
            left[pl.ds(a, chan, stride=rows), :].T.astype(bf16))
        out_ref[RADIX * a + 128 : RADIX * (a + 1), :] = (
            right[pl.ds(a, chan, stride=rows), :].T.astype(bf16))


def forward_kernel(per, rows, block, r_ref, first_ref, twf_ref, row0_ref, second_ref, last_in_ref,
                   cin_ref, cout_in_ref, bias_in_ref, skip_in_ref,
                   feat_ref, spec_ref, nyq_ref, last_ref, cout_ref, bias_ref, skip_ref,
                   hi, lo, hi2, lo2):
    last_ref[...] = last_in_ref[...]
    cout_ref[...] = cout_in_ref[...]
    bias_ref[...] = jnp.broadcast_to(bias_in_ref[...], bias_ref.shape)
    skip_ref[...] = jnp.broadcast_to(skip_in_ref[...], skip_ref.shape)
    pieces = feat_ref.shape[0]
    values = r_ref[...].astype(f32)
    first_row = iota((8, RADIX), 0) == 0
    spare = jnp.zeros((8, 128), f32)
    spare_lane = iota((8, 128), 1)
    for c in range(per):
        x = values[:, block * c : block * (c + 1), :].reshape(RADIX, RADIX).astype(bf16)
        a = mm(first_ref[...], x)
        a = a[:RADIX] + a[RADIX:]
        re, im = a[:HALF], a[HALF:]
        out_re = re * twf_ref[0] + im * twf_ref[1]
        out_im = im * twf_ref[2] - re * twf_ref[1]
        place = pl.ds(HALF * c, HALF)
        for at, part in ((0, out_re), (RADIX, out_im)):
            high, low = split(part)
            hi[place, at : at + RADIX], lo[place, at : at + RADIX] = high, low
            hi2[place, at : at + RADIX], lo2[place, at : at + RADIX] = high, low
        lead = im[0:8]
        top = pl.ds(HALF * c, 16)
        alt_re = jnp.concatenate(
            [jnp.where(first_row, lead * row0_ref[0], out_re[0:8]), out_re[8:16]], 0)
        alt_im = jnp.concatenate(
            [jnp.where(first_row, -lead * row0_ref[1], out_im[0:8]), out_im[8:16]], 0)
        for at, part in ((0, alt_re), (RADIX, alt_im)):
            high, low = split(part)
            hi2[top, at : at + RADIX], lo2[top, at : at + RADIX] = high, low
        nyq = jnp.sum(re[0:1] * row0_ref[2, 0:1], axis=1, keepdims=True)
        spare = jnp.where(spare_lane == c, nyq, spare)
    nyq_ref[...] = spare
    chan = cin_ref.shape[1]
    own = (lax.axis_index("chip") * lax.axis_size("core") + lax.axis_index("core")) * per
    row = iota((8, chan), 0)
    select = ((iota((8, chan), 1) == own + row) & (row < per)).astype(f32).astype(bf16)
    tile = jnp.concatenate([nt(select, cin_ref[...]) * IN_SCALE,
                            nt(select, cout_in_ref[...]) * OUT_SCALE], 1)
    tile = jnp.where(iota((8, 128), 0) == per, jnp.log1p(spare * spare * (1.0 / SEQ)), tile)
    width = HALF * per
    feat_ref[:, :, width:] = jnp.broadcast_to(tile[None], (pieces, rows, 128))
    for part, (h, l) in enumerate(((hi, lo), (hi2, lo2))):
        s = (nt(second_ref[0, part], h[...]) + nt(second_ref[0, part], l[...])
             + nt(second_ref[1, part], h[...]))
        spec_ref[part] = s
        re, im = s[:HALF], s[HALF:]
        feature = jnp.log1p((re * re + im * im) * (1.0 / SEQ))
        count = HALF // rows
        feat_ref[part * count : (part + 1) * count, :, :width] = feature.reshape(
            count, rows, width)


def reduce_kernel(per, rows, hid, f_ref, out_ref, tile_ref):
    pieces = f_ref.shape[0]
    groups = out_ref.shape[0]
    chunk = pieces * rows
    tile = f_ref[:, :, HALF * per :]
    tile_ref[...] = tile
    lane = iota((hid, chunk), 1) % rows
    weights, features = [], []
    for c in range(per):
        spread = jnp.broadcast_to(tile[:, c : c + 1, :], tile.shape).reshape(chunk, 128)
        spread = spread.T[:hid]
        weights.append(jnp.concatenate(
            [jnp.where(lane == k, spread, 0.0) for k in range(rows)], 0).astype(bf16))
        features.append(f_ref[:, :, HALF * c : HALF * (c + 1)].reshape(chunk, HALF))
    high, low = split(jnp.concatenate(features, 0))
    pre = mm(jnp.concatenate(weights, 1), jnp.concatenate([high, low], 1))
    pre = (pre[:, :HALF] + pre[:, HALF:]) * (1.0 / IN_SCALE)
    main = pre.shape[0] // groups
    out_ref[:, :main, :] = pre.reshape(groups, main, HALF)
    extra = jnp.zeros((pieces, 128), f32)
    for c in range(per):
        extra = extra + tile[:, c, :] * tile[:, per, c : c + 1]
    extra = jnp.sum(extra, axis=0, keepdims=True) * (1.0 / IN_SCALE)
    out_ref[:, main:, :] = jnp.broadcast_to(extra[None], (groups, 8, 128))


def gelu(v):
    return 0.5 * v * (1.0 + lax.erf(v * math.sqrt(0.5)))


def hidden_kernel(main, hid, r_ref, bias_ref, cout_ref, out_ref, gain_ref):
    groups = r_ref.shape[0]
    total = r_ref[0]
    for g in range(1, groups):
        total = total + r_ref[g]
    start = lax.axis_index("chip") * main
    bias = bias_ref[0:1]
    column = jnp.sum(
        jnp.where(iota((main, hid), 1) == (iota((main, hid), 0) + start) % hid, bias, 0.0),
        axis=1, keepdims=True)
    out_ref[...] = gelu(total[:main] + column)
    spare = gelu(total[main:, :hid] + bias)
    high, low = split(spare)
    gain_ref[...] = mm(high, cout_ref[...]) + mm(low, cout_ref[...])


def gain_kernel(per, rows, hid, h_ref, tile_ref, out_ref):
    pieces = tile_ref.shape[0]
    chunk = pieces * rows
    wide = rows * hid
    high, low = split(h_ref[...].reshape(wide, HALF))
    hidden = jnp.concatenate([high, low], 1)
    keep = iota((chunk, wide), 0) % rows == iota((chunk, wide), 1) // hid
    tile = tile_ref[...]
    for c in range(per):
        spread = jnp.broadcast_to(tile[:, c : c + 1, :], tile.shape).reshape(chunk, 128)
        spread = jnp.concatenate([spread[:, hid:]] * rows, 1)
        g = mm(jnp.where(keep, spread, 0.0).astype(bf16), hidden)
        g = (g[:, :HALF] + g[:, HALF:]) * (GAIN_SCALE / OUT_SCALE)
        out_ref[:, :, HALF * c : HALF * (c + 1)] = g.reshape(pieces, rows, HALF)


def inverse_kernel(per, block, g_ref, spec_ref, nyq_ref, gain_ref, skip_ref, r_ref,
                   inv_ref, twf_ref, last_ref, row0_ref, out_ref):
    members = r_ref.shape[0]
    width = HALF * per
    count = g_ref.shape[0] // 2
    sums = []
    for part in range(2):
        g = g_ref[part * count : (part + 1) * count].reshape(HALF, width)
        g = g * (1.0 / GAIN_SCALE)
        if part == 0:
            dc = (iota((HALF, width), 0) == 0) & (iota((HALF, width), 1) % HALF == 0)
            g = jnp.where(dc, 0.5 * g, g)
        s = spec_ref[part]
        high, low = split(jnp.concatenate([s[:HALF] * g, s[HALF:] * g], 0))
        sums.append(mm(inv_ref[0, part], high) + mm(inv_ref[0, part], low)
                    + mm(inv_ref[1, part], high))
    own = (lax.axis_index("chip") * lax.axis_size("core") + lax.axis_index("core")) * per
    lane = iota((1, 128), 1)
    cosine, sine = twf_ref[0].T, twf_ref[1].T
    shared_cos, shared_sin = row0_ref[0].T[:, 0:1], row0_ref[1].T[:, 0:1]
    lane0 = iota((RADIX, HALF), 1) == 0
    outs = []
    for c in range(per):
        cols = slice(HALF * c, HALF * (c + 1))
        top_re, top_im = sums[0][:RADIX, cols], sums[0][RADIX:, cols]
        bot_re, bot_im = sums[1][:RADIX, cols], sums[1][RADIX:, cols]
        re = jnp.where(lane0, top_re, top_re + bot_re)
        im = top_im + bot_im
        out_re = jnp.where(lane0, re, re * cosine - im * sine)
        out_im = jnp.where(lane0, bot_re * shared_cos - bot_im * shared_sin,
                           re * sine + im * cosine)
        high, low = split(jnp.concatenate([out_re, out_im], 1))
        y = nt(last_ref[0], high) + nt(last_ref[0], low) + nt(last_ref[1], high)
        mine = lane == own + c
        skip = jnp.sum(jnp.where(mine, skip_ref[0:1], 0.0), axis=1, keepdims=True)
        gain = jnp.sum(jnp.where(mine, gain_ref[0:1], 0.0), axis=1, keepdims=True)
        spare = jnp.sum(jnp.where(lane == c, nyq_ref[0:1], 0.0), axis=1, keepdims=True)
        x = r_ref[:, block * c : block * (c + 1), :].astype(f32).reshape(RADIX, RADIX)
        y = y + (spare * gain * (1.0 / SEQ)) * row0_ref[2, 0:1] + skip * x
        outs.append(y.reshape(members, block, RADIX))
    out_ref[...] = jnp.concatenate(outs, 1).astype(bf16)


def call(kernel, outs, scratch=(), flops=0, interpret=False):
    vmem = pl.BlockSpec(memory_space=pltpu.VMEM)
    many = isinstance(outs, (list, tuple))

    def run(*args):
        return pl.pallas_call(
            kernel,
            out_shape=outs,
            in_specs=[vmem] * len(args),
            out_specs=[vmem] * len(outs) if many else vmem,
            scratch_shapes=list(scratch),
            compiler_params=pltpu.CompilerParams(vmem_limit_bytes=40 * 1024 * 1024),
        )(*args)

    return run


def exchange(x, axis):
    return lax.all_to_all(x, axis, split_axis=0, concat_axis=0, tiled=True)


def on_device(signal, cond_in, cond_bias, cond_out, skip_gain):
    shape = jax.ShapeDtypeStruct
    ctx, other = ("chip", "core"), ("core", "ch")
    members = lax.axis_size(ctx)
    pieces = lax.axis_size(other)
    groups = lax.axis_size("chip")
    seq_local, chan = signal.shape
    hid = cond_in.shape[1]
    per = chan // members
    rows = RADIX // pieces
    block = seq_local // RADIX
    width = HALF * per
    t = {name: jnp.asarray(value) for name, value in tables().items()}
    halves = [pltpu.VMEM((chan * block, 128), f32)] * 2
    piece = shape((members, per * block, RADIX), bf16)

    packed = call(pack_kernel, piece, halves)(signal)
    received = exchange(packed, ctx)
    feat, spec, nyq, last, cout, bias, skip = call(
        functools.partial(forward_kernel, per, rows, block),
        [shape((pieces, rows, width + 128), f32), shape((2, RADIX, width), f32),
         shape((8, 128), f32), shape((2, RADIX, RADIX), bf16), shape((hid, chan), bf16),
         shape((8, hid), f32), shape((8, chan), f32)],
        [pltpu.VMEM((width, 2 * RADIX), bf16)] * 4)(
            received, t["first"], t["twf"], t["row0"], t["second"], t["last"],
            cond_in.T, cond_out, cond_bias.reshape(1, hid), skip_gain.reshape(1, chan))
    feat = exchange(feat.astype(f16), other).astype(f32)
    main = rows * hid // groups
    partial, tile = call(functools.partial(reduce_kernel, per, rows, hid),
                         [shape((groups, main + 8, HALF), f32),
                          shape((pieces, rows, 128), f32)])(feat)
    partial = exchange(partial.astype(f16), "chip").astype(f32)
    hidden, spare_gain = call(functools.partial(hidden_kernel, main, hid),
                              [shape((main, HALF), f32), shape((8, chan), f32)])(
                                  partial, bias, cout)
    hidden = jnp.broadcast_to(hidden.astype(f16)[None], (groups, main, HALF))
    hidden = exchange(hidden, "chip").astype(f32)
    gain = call(functools.partial(gain_kernel, per, rows, hid),
                shape((pieces, rows, width), f32))(hidden, tile)
    gain = exchange(gain.astype(f16), other).astype(f32)
    mixed = call(functools.partial(inverse_kernel, per, block), piece)(
        gain, spec, nyq, spare_gain, skip, received, t["inv"], t["twf"], last, t["row0"])
    mixed = exchange(mixed, ctx)
    return call(unpack_kernel, shape((seq_local, chan), bf16), halves)(mixed)


def solution(mesh):
    devices = mesh.devices
    cores = 2
    fine = Mesh(devices.reshape(devices.shape[0] // cores, cores, devices.shape[1]),
                ("chip", "core", "ch"))
    ctx = ("chip", "core")
    return jax.shard_map(
        on_device,
        mesh=fine,
        in_specs=(P(ctx, "ch"), P("ch", None), P(), P(None, "ch"), P("ch")),
        out_specs=P(ctx, "ch"),
        check_vma=False,
    )
```

```python
import functools
import math

import jax
import jax.numpy as jnp
import numpy as np
from jax import lax
from jax.experimental import pallas as pl
from jax.experimental.pallas import tpu as pltpu
from jax.sharding import Mesh
from jax.sharding import PartitionSpec as P

f32, bf16, f16 = jnp.float32, jnp.bfloat16, jnp.float16

RADIX = 256
HALF = RADIX // 2
SEQ = RADIX * RADIX
STEP = 2
TILE = 8
GAIN_SCALE = 0.25
IN_SCALE = 2.0**18
OUT_SCALE = 2.0**16


def split_const(values):
    high = values.astype(np.float32).astype(jnp.bfloat16)
    low = (values - high.astype(np.float64)).astype(np.float32).astype(jnp.bfloat16)
    return high, low


@functools.lru_cache(maxsize=None)
def tables():
    n = np.arange(RADIX, dtype=np.float64)
    k = np.arange(HALF, dtype=np.float64)
    tau = 2.0 * np.pi
    angle = tau * np.outer(k, n) / RADIX
    first = np.concatenate([np.cos(angle), -np.sin(angle)], 0)
    first[HALF] = np.cos(math.pi * n)
    first = np.concatenate(split_const(first), 0)
    angle = tau * np.outer(k, n) / SEQ
    cos_f, sin_f = np.cos(angle), np.sin(angle)
    cos_g = cos_f.copy()
    cos_g[0] = 0.0
    shared = tau * n * (HALF + SEQ // 2) / SEQ
    twf = np.stack([cos_f, sin_f, cos_g]).astype(np.float32)
    row0 = np.zeros((3, 8, RADIX))
    row0[0, 0], row0[1, 0] = np.cos(shared), np.sin(shared)
    row0[2, :] = np.cos(math.pi * n)
    row0 = row0.astype(np.float32)
    angle = tau * np.outer(n, n) / RADIX
    wre, wim = np.cos(angle), -np.sin(angle)
    full = [np.concatenate([wre, -wim], 1), np.concatenate([wim, wre], 1)]
    order = np.arange(HALF).reshape(-1, STEP).T.reshape(-1)
    second = np.stack([np.concatenate([f[order] for f in full], 0),
                       np.concatenate([f[HALF + order] for f in full], 0)])
    second = np.stack(split_const(second))
    vre, vim = np.cos(angle), np.sin(angle)
    inv = np.stack([
        np.concatenate([np.concatenate([vre[:, s], -vim[:, s]], 1),
                        np.concatenate([vim[:, s], vre[:, s]], 1)], 0)
        for s in (order, HALF + order)])
    inv = np.stack(split_const(inv))
    angle = tau * np.outer(n, k) / RADIX
    last = np.concatenate([np.cos(angle), -np.sin(angle)], 1)
    last[:, HALF] = np.cos(math.pi * n)
    last = np.stack(split_const(last * (2.0 / SEQ)))
    return dict(first=first, twf=twf, row0=row0, second=second, inv=inv, last=last)


def split(x):
    high = x.astype(bf16)
    return high, (x - high.astype(f32)).astype(bf16)


def mm(a, b):
    return jnp.dot(a, b, preferred_element_type=f32)


def nt(a, b):
    return lax.dot_general(a, b, (((1,), (1,)), ((), ())), preferred_element_type=f32)


def iota(shape, axis):
    return lax.broadcasted_iota(jnp.int32, shape, axis)


def first_channel(per):
    index = lax.axis_index("xh") * lax.axis_size("y") + lax.axis_index("y")
    return (index * lax.axis_size("core") + lax.axis_index("core")) * per


def pack_kernel(x_ref, out_ref, left, right):
    rows = x_ref.shape[0] // RADIX
    chan = x_ref.shape[1]
    for a in range(rows):
        block = x_ref[RADIX * a : RADIX * (a + 1), :].astype(f32).T
        left[pl.ds(a, chan, stride=rows), :] = block[:, :128]
        right[pl.ds(a, chan, stride=rows), :] = block[:, 128:]
    out_ref[:, :, :128] = left[...].astype(bf16).reshape(out_ref.shape[:2] + (128,))
    out_ref[:, :, 128:] = right[...].astype(bf16).reshape(out_ref.shape[:2] + (128,))


def unpack_kernel(r_ref, out_ref, left, right):
    rows = out_ref.shape[0] // RADIX
    chan = out_ref.shape[1]
    left[...] = r_ref[:, :, :128].astype(f32).reshape(left.shape)
    right[...] = r_ref[:, :, 128:].astype(f32).reshape(right.shape)
    for a in range(rows):
        out_ref[RADIX * a : RADIX * a + 128, :] = (
            left[pl.ds(a, chan, stride=rows), :].T.astype(bf16))
        out_ref[RADIX * a + 128 : RADIX * (a + 1), :] = (
            right[pl.ds(a, chan, stride=rows), :].T.astype(bf16))


def forward_kernel(per, block, r_ref, first_ref, twf_ref, row0_ref, second_ref, last_in_ref,
                   cin_ref, cout_in_ref, bias_in_ref, skip_in_ref,
                   feat_ref, spec_ref, nyq_ref, last_ref, cout_ref, bias_ref, skip_ref,
                   hi, lo, hi2, lo2):
    last_ref[...] = last_in_ref[...]
    cout_ref[...] = cout_in_ref[...]
    bias_ref[...] = jnp.broadcast_to(bias_in_ref[...], bias_ref.shape)
    skip_ref[...] = jnp.broadcast_to(skip_in_ref[...], skip_ref.shape)
    values = r_ref[...].astype(f32)
    first_row = iota((8, RADIX), 0) == 0
    spare = jnp.zeros((8, 128), f32)
    spare_lane = iota((8, 128), 1)
    for c in range(per):
        x = values[:, block * c : block * (c + 1), :].reshape(RADIX, RADIX).astype(bf16)
        a = mm(first_ref[...], x)
        a = a[:RADIX] + a[RADIX:]
        re, im = a[:HALF], a[HALF:]
        out_re = re * twf_ref[0] + im * twf_ref[1]
        out_im = im * twf_ref[2] - re * twf_ref[1]
        place = pl.ds(HALF * c, HALF)
        for at, part in ((0, out_re), (RADIX, out_im)):
            high, low = split(part)
            hi[place, at : at + RADIX], lo[place, at : at + RADIX] = high, low
            hi2[place, at : at + RADIX], lo2[place, at : at + RADIX] = high, low
        lead = im[0:8]
        top = pl.ds(HALF * c, 16)
        alt_re = jnp.concatenate(
            [jnp.where(first_row, lead * row0_ref[0], out_re[0:8]), out_re[8:16]], 0)
        alt_im = jnp.concatenate(
            [jnp.where(first_row, -lead * row0_ref[1], out_im[0:8]), out_im[8:16]], 0)
        for at, part in ((0, alt_re), (RADIX, alt_im)):
            high, low = split(part)
            hi2[top, at : at + RADIX], lo2[top, at : at + RADIX] = high, low
        nyq = jnp.sum(re[0:1] * row0_ref[2, 0:1], axis=1, keepdims=True)
        spare = jnp.where(spare_lane == c, nyq, spare)
    nyq_ref[...] = spare
    chan = cin_ref.shape[1]
    row = iota((TILE, chan), 0)
    select = ((iota((TILE, chan), 1) == first_channel(per) + row) & (row < per))
    select = select.astype(f32).astype(bf16)
    tile = jnp.concatenate([nt(select, cin_ref[...]) * IN_SCALE,
                            nt(select, cout_in_ref[...]) * OUT_SCALE], 1)
    tile = jnp.where(iota((TILE, 128), 0) == per, jnp.log1p(spare * spare * (1.0 / SEQ)), tile)
    stride = 2 * TILE
    pieces = feat_ref.shape[0] // stride
    for r in range(TILE):
        feat_ref[pl.ds(TILE + r, pieces, stride=stride), :] = jnp.broadcast_to(
            tile[r : r + 1], (pieces, 128))
    count = HALF // STEP
    for part, (h, l) in enumerate(((hi, lo), (hi2, lo2))):
        s = (nt(second_ref[0, part], h[...]) + nt(second_ref[0, part], l[...])
             + nt(second_ref[1, part], h[...]))
        spec_ref[part] = s
        re, im = s[:HALF], s[HALF:]
        feature = jnp.log1p((re * re + im * im) * (1.0 / SEQ))
        for c in range(per):
            for k in range(STEP):
                feat_ref[pl.ds(part * count * stride + STEP * c + k, count, stride=stride), :] = (
                    feature[count * k : count * (k + 1), HALF * c : HALF * (c + 1)])


def reduce_kernel(per, hid, f_ref, out_ref):
    stride = 2 * TILE
    pieces = f_ref.shape[0] // stride

    def rows(r):
        return f_ref[pl.ds(r, pieces, stride=stride), :]

    weights = [rows(TILE + c) for c in range(per)]
    left = jnp.concatenate([w.T[:hid] for w in weights], 1).astype(bf16)
    features = jnp.concatenate(
        [jnp.concatenate([rows(STEP * c + k) for c in range(per)], 0) for k in range(STEP)], 1)
    high, low = split(features)
    pre = mm(left, jnp.concatenate([high, low], 1))
    width = STEP * HALF
    out_ref[:hid] = (pre[:, :width] + pre[:, width:]) * (1.0 / IN_SCALE)
    last = rows(TILE + per)
    extra = weights[0] * last[:, 0:1]
    for c in range(1, per):
        extra = extra + weights[c] * last[:, c : c + 1]
    extra = jnp.sum(extra, axis=0, keepdims=True) * (1.0 / IN_SCALE)
    out_ref[hid:, :128] = jnp.broadcast_to(extra, (TILE, 128))
    out_ref[hid:, 128:] = jnp.zeros((TILE, width - 128), f32)


def gelu(v):
    return 0.5 * v * (1.0 + lax.erf(v * math.sqrt(0.5)))


def gain_kernel(per, hid, r_ref, f_ref, bias_ref, cout_ref, out_ref, gain_ref):
    total = r_ref[0]
    for g in range(1, r_ref.shape[0]):
        total = total + r_ref[g]
    bias = bias_ref[0:1]
    column = jnp.sum(jnp.where(iota((hid, hid), 1) == iota((hid, hid), 0), bias, 0.0),
                     axis=1, keepdims=True)
    high, low = split(gelu(total[:hid] + column))
    hidden = jnp.concatenate([high, low], 1)
    hidden = jnp.concatenate([jnp.zeros_like(hidden), hidden], 0)
    stride = 2 * TILE
    pieces = f_ref.shape[0] // stride
    width = STEP * HALF
    for c in range(per):
        weights = f_ref[pl.ds(TILE + c, pieces, stride=stride), :].astype(bf16)
        g = mm(weights, hidden)
        g = (g[:, :width] + g[:, width:]) * (GAIN_SCALE / OUT_SCALE)
        for k in range(STEP):
            out_ref[pl.ds(STEP * c + k, pieces, stride=TILE), :] = g[:, HALF * k : HALF * (k + 1)]
    high, low = split(gelu(total[hid:, :hid] + bias))
    gain_ref[...] = mm(high, cout_ref[...]) + mm(low, cout_ref[...])


def inverse_kernel(per, block, g_ref, spec_ref, nyq_ref, gain_ref, skip_ref, r_ref,
                   inv_ref, twf_ref, last_ref, row0_ref, out_ref):
    members = r_ref.shape[0]
    width = HALF * per
    count = HALF // STEP
    sums = []
    for part in range(2):
        g = jnp.concatenate([
            jnp.concatenate([
                g_ref[pl.ds(part * count * TILE + STEP * c + k, count, stride=TILE), :]
                for k in range(STEP)], 0)
            for c in range(per)], 1) * (1.0 / GAIN_SCALE)
        if part == 0:
            dc = (iota((HALF, width), 0) == 0) & (iota((HALF, width), 1) % HALF == 0)
            g = jnp.where(dc, 0.5 * g, g)
        s = spec_ref[part]
        high, low = split(jnp.concatenate([s[:HALF] * g, s[HALF:] * g], 0))
        sums.append(mm(inv_ref[0, part], high) + mm(inv_ref[0, part], low)
                    + mm(inv_ref[1, part], high))
    own = first_channel(per)
    lane = iota((1, 128), 1)
    cosine, sine = twf_ref[0].T, twf_ref[1].T
    shared_cos, shared_sin = row0_ref[0].T[:, 0:1], row0_ref[1].T[:, 0:1]
    lane0 = iota((RADIX, HALF), 1) == 0
    outs = []
    for c in range(per):
        cols = slice(HALF * c, HALF * (c + 1))
        top_re, top_im = sums[0][:RADIX, cols], sums[0][RADIX:, cols]
        bot_re, bot_im = sums[1][:RADIX, cols], sums[1][RADIX:, cols]
        re = jnp.where(lane0, top_re, top_re + bot_re)
        im = top_im + bot_im
        out_re = jnp.where(lane0, re, re * cosine - im * sine)
        out_im = jnp.where(lane0, bot_re * shared_cos - bot_im * shared_sin,
                           re * sine + im * cosine)
        high, low = split(jnp.concatenate([out_re, out_im], 1))
        y = nt(last_ref[0], high) + nt(last_ref[0], low) + nt(last_ref[1], high)
        mine = lane == own + c
        skip = jnp.sum(jnp.where(mine, skip_ref[0:1], 0.0), axis=1, keepdims=True)
        gain = jnp.sum(jnp.where(mine, gain_ref[0:1], 0.0), axis=1, keepdims=True)
        spare = jnp.sum(jnp.where(lane == c, nyq_ref[0:1], 0.0), axis=1, keepdims=True)
        x = r_ref[:, block * c : block * (c + 1), :].astype(f32).reshape(RADIX, RADIX)
        y = y + (spare * gain * (1.0 / SEQ)) * row0_ref[2, 0:1] + skip * x
        outs.append(y.reshape(members, block, RADIX))
    out_ref[...] = jnp.concatenate(outs, 1).astype(bf16)


def call(kernel, outs, scratch=(), flops=0, interpret=False):
    vmem = pl.BlockSpec(memory_space=pltpu.VMEM)
    many = isinstance(outs, (list, tuple))

    def run(*args):
        return pl.pallas_call(
            kernel,
            out_shape=outs,
            in_specs=[vmem] * len(args),
            out_specs=[vmem] * len(outs) if many else vmem,
            scratch_shapes=list(scratch),
            compiler_params=pltpu.CompilerParams(vmem_limit_bytes=40 * 1024 * 1024),
        )(*args)

    return run


def exchange(x, axis):
    return lax.all_to_all(x, axis, split_axis=0, concat_axis=0, tiled=True)


def on_device(signal, cond_in, cond_bias, cond_out, skip_gain):
    shape = jax.ShapeDtypeStruct
    ctx, spread, line = ("xh", "y", "core"), ("y", "core", "z"), ("xh", "xl")
    members = lax.axis_size(ctx)
    pieces = lax.axis_size(spread)
    groups = lax.axis_size(line)
    seq_local, chan = signal.shape
    hid = cond_in.shape[1]
    per = chan // members
    block = seq_local // RADIX
    width = HALF * per
    t = {name: jnp.asarray(value) for name, value in tables().items()}
    halves = [pltpu.VMEM((chan * block, 128), f32)] * 2
    piece = shape((members, per * block, RADIX), bf16)

    def send(x, axis, count):
        x = x.astype(f16).reshape(count, -1, x.shape[-1])
        return exchange(x, axis).astype(f32)

    packed = call(pack_kernel, piece, halves)(signal)
    received = exchange(packed, ctx)
    feat, spec, nyq, last, cout, bias, skip = call(
        functools.partial(forward_kernel, per, block),
        [shape((pieces * 2 * TILE, HALF), f32), shape((2, RADIX, width), f32),
         shape((8, 128), f32), shape((2, RADIX, RADIX), bf16), shape((hid, chan), bf16),
         shape((8, hid), f32), shape((8, chan), f32)],
        [pltpu.VMEM((width, 2 * RADIX), bf16)] * 4)(
            received, t["first"], t["twf"], t["row0"], t["second"], t["last"],
            cond_in.T, cond_out, cond_bias.reshape(1, hid), skip_gain.reshape(1, chan))
    feat = send(feat, spread, pieces).reshape(feat.shape)
    partial = call(functools.partial(reduce_kernel, per, hid),
                   shape((hid + TILE, STEP * HALF), f32))(feat)
    partial = jnp.broadcast_to(partial[None], (groups,) + partial.shape)
    partial = send(partial, line, groups)
    gain, spare_gain = call(functools.partial(gain_kernel, per, hid),
                            [shape((pieces * TILE, HALF), f32), shape((8, chan), f32)])(
                                partial, feat, bias, cout)
    gain = send(gain, spread, pieces).reshape(gain.shape)
    mixed = call(functools.partial(inverse_kernel, per, block), piece)(
        gain, spec, nyq, spare_gain, skip, received, t["inv"], t["twf"], last, t["row0"])
    mixed = exchange(mixed, ctx)
    return call(unpack_kernel, shape((seq_local, chan), bf16), halves)(mixed)


def solution(mesh):
    fine = Mesh(mesh.devices.reshape(2, -1, 2, 2, mesh.devices.shape[1] // 2),
                ("xh", "y", "core", "xl", "z"))
    ctx, ch = ("xh", "y", "core"), ("xl", "z")
    return jax.shard_map(
        on_device,
        mesh=fine,
        in_specs=(P(ctx, ch), P(ch, None), P(), P(None, ch), P(ch)),
        out_specs=P(ctx, ch),
        check_vma=False,
    )
```

```python
import functools
import math

import jax
import jax.numpy as jnp
import numpy as np
from jax import lax
from jax.experimental import pallas as pl
from jax.experimental.pallas import tpu as pltpu
from jax.sharding import Mesh
from jax.sharding import PartitionSpec as P

f32, bf16, f16 = jnp.float32, jnp.bfloat16, jnp.float16

RADIX = 256
HALF = RADIX // 2
SEQ = RADIX * RADIX
STEP = 2
TILE = 8
GAIN_SCALE = 0.25
IN_SCALE = 2.0**18
OUT_SCALE = 2.0**16


def split_const(values):
    high = values.astype(np.float32).astype(jnp.bfloat16)
    low = (values - high.astype(np.float64)).astype(np.float32).astype(jnp.bfloat16)
    return high, low


@functools.lru_cache(maxsize=None)
def tables(sizes):
    arrival = np.arange(math.prod(sizes)).reshape(sizes).transpose(1, 0, 2).reshape(-1)
    block = RADIX // arrival.size
    position = (arrival[:, None] * block + np.arange(block)).reshape(-1)
    n = np.arange(RADIX, dtype=np.float64)
    k = np.arange(HALF, dtype=np.float64)
    tau = 2.0 * np.pi
    angle = tau * np.outer(k, n) / RADIX
    first = np.concatenate([np.cos(angle), -np.sin(angle)], 0)
    first[HALF] = np.cos(math.pi * n)
    first = np.concatenate(split_const(first[:, position]), 0)
    angle = tau * np.outer(k, n) / SEQ
    cos_f, sin_f = np.cos(angle), np.sin(angle)
    cos_g = cos_f.copy()
    cos_g[0] = 0.0
    shared = tau * n * (HALF + SEQ // 2) / SEQ
    twf = np.stack([cos_f, sin_f, cos_g]).astype(np.float32)
    row0 = np.zeros((3, 8, RADIX))
    row0[0, 0], row0[1, 0] = np.cos(shared), np.sin(shared)
    row0[2, :] = np.cos(math.pi * n)
    row0 = row0.astype(np.float32)
    angle = tau * np.outer(n, n) / RADIX
    wre, wim = np.cos(angle), -np.sin(angle)
    full = [np.concatenate([wre, -wim], 1), np.concatenate([wim, wre], 1)]
    order = np.arange(HALF).reshape(-1, STEP).T.reshape(-1)
    second = np.stack([np.concatenate([f[order] for f in full], 0),
                       np.concatenate([f[HALF + order] for f in full], 0)])
    second = np.stack(split_const(second))
    vre, vim = np.cos(angle), np.sin(angle)
    inv = np.stack([
        np.concatenate([np.concatenate([vre[:, s], -vim[:, s]], 1),
                        np.concatenate([vim[:, s], vre[:, s]], 1)], 0)
        for s in (order, HALF + order)])
    inv = np.stack(split_const(inv))
    angle = tau * np.outer(n, k) / RADIX
    last = np.concatenate([np.cos(angle), -np.sin(angle)], 1)
    last[:, HALF] = np.cos(math.pi * n)
    last = np.stack(split_const(last[position] * (2.0 / SEQ)))
    return dict(first=first, twf=twf, row0=row0, second=second, inv=inv, last=last)


def split(x):
    high = x.astype(bf16)
    return high, (x - high.astype(f32)).astype(bf16)


def mm(a, b):
    return jnp.dot(a, b, preferred_element_type=f32)


def nt(a, b):
    return lax.dot_general(a, b, (((1,), (1,)), ((), ())), preferred_element_type=f32)


def iota(shape, axis):
    return lax.broadcasted_iota(jnp.int32, shape, axis)


def first_channel(per):
    index = lax.axis_index("y") * lax.axis_size("xh") + lax.axis_index("xh")
    return (index * lax.axis_size("core") + lax.axis_index("core")) * per


def pack_kernel(x_ref, bias_ref, skip_ref, out_ref, bias_out, skip_out, left, right, x, sems):
    blocks = x_ref.shape[0] // RADIX
    chan = x_ref.shape[1]

    def rows(a):
        return pl.ds(RADIX * a, RADIX)

    copies = [pltpu.make_async_copy(x_ref.at[rows(a)], x.at[rows(a)], sems.at[a])
              for a in range(blocks)]
    copies += [pltpu.make_async_copy(bias_ref, bias_out, sems.at[blocks]),
               pltpu.make_async_copy(skip_ref, skip_out, sems.at[blocks + 1])]
    for copy in copies:
        copy.start()
    for a in range(blocks):
        copies[a].wait()
        block = x[RADIX * a : RADIX * (a + 1), :].astype(f32).T
        left[pl.ds(a, chan, stride=blocks), :] = block[:, :128]
        right[pl.ds(a, chan, stride=blocks), :] = block[:, 128:]
    out_ref[:, :, :128] = left[...].astype(bf16).reshape(out_ref.shape[:2] + (128,))
    out_ref[:, :, 128:] = right[...].astype(bf16).reshape(out_ref.shape[:2] + (128,))
    for copy in copies[blocks:]:
        copy.wait()


def unpack_kernel(r_ref, out_ref, left, right, y, sems):
    blocks = out_ref.shape[0] // RADIX
    chan = out_ref.shape[1]
    left[...] = r_ref[:, :, :128].astype(f32).reshape(left.shape)
    right[...] = r_ref[:, :, 128:].astype(f32).reshape(right.shape)
    copies = []
    for a in range(blocks):
        y[RADIX * a : RADIX * a + 128, :] = (
            left[pl.ds(a, chan, stride=blocks), :].T.astype(bf16))
        y[RADIX * a + 128 : RADIX * (a + 1), :] = (
            right[pl.ds(a, chan, stride=blocks), :].T.astype(bf16))
        rows = pl.ds(RADIX * a, RADIX)
        copies.append(pltpu.make_async_copy(y.at[rows], out_ref.at[rows], sems.at[a]))
        copies[-1].start()
    for copy in copies:
        copy.wait()


def forward_kernel(per, block, r_ref, first_ref, twf_ref, row0_ref, second_ref, last_in_ref,
                   cin_ref, cout_in_ref, feat_ref, spec_ref, nyq_ref, last_ref, cout_ref,
                   hi, lo, hi2, lo2):
    last_ref[...] = last_in_ref[...]
    cout_ref[...] = cout_in_ref[...]
    values = r_ref[...].astype(f32)
    first_row = iota((8, RADIX), 0) == 0
    spare = jnp.zeros((8, 128), f32)
    spare_lane = iota((8, 128), 1)
    for c in range(per):
        x = values[:, block * c : block * (c + 1), :].reshape(RADIX, RADIX).astype(bf16)
        a = mm(first_ref[...], x)
        a = a[:RADIX] + a[RADIX:]
        re, im = a[:HALF], a[HALF:]
        out_re = re * twf_ref[0] + im * twf_ref[1]
        out_im = im * twf_ref[2] - re * twf_ref[1]
        place = pl.ds(HALF * c, HALF)
        for at, part in ((0, out_re), (RADIX, out_im)):
            high, low = split(part)
            hi[place, at : at + RADIX], lo[place, at : at + RADIX] = high, low
            hi2[place, at : at + RADIX], lo2[place, at : at + RADIX] = high, low
        lead = im[0:8]
        top = pl.ds(HALF * c, 16)
        alt_re = jnp.concatenate(
            [jnp.where(first_row, lead * row0_ref[0], out_re[0:8]), out_re[8:16]], 0)
        alt_im = jnp.concatenate(
            [jnp.where(first_row, -lead * row0_ref[1], out_im[0:8]), out_im[8:16]], 0)
        for at, part in ((0, alt_re), (RADIX, alt_im)):
            high, low = split(part)
            hi2[top, at : at + RADIX], lo2[top, at : at + RADIX] = high, low
        nyq = jnp.sum(re[0:1] * row0_ref[2, 0:1], axis=1, keepdims=True)
        spare = jnp.where(spare_lane == c, nyq, spare)
    nyq_ref[...] = spare
    chan = cin_ref.shape[1]
    row = iota((TILE, chan), 0)
    select = ((iota((TILE, chan), 1) == first_channel(per) + row) & (row < per))
    select = select.astype(f32).astype(bf16)
    tile = jnp.concatenate([nt(select, cin_ref[...]) * IN_SCALE,
                            nt(select, cout_in_ref[...]) * OUT_SCALE], 1)
    tile = jnp.where(iota((TILE, 128), 0) == per, jnp.log1p(spare * spare * (1.0 / SEQ)), tile)
    stride = 2 * TILE
    pieces = feat_ref.shape[0] // stride
    for r in range(TILE):
        feat_ref[pl.ds(TILE + r, pieces, stride=stride), :] = jnp.broadcast_to(
            tile[r : r + 1], (pieces, 128))
    count = HALF // STEP
    for part, (h, l) in enumerate(((hi, lo), (hi2, lo2))):
        s = (nt(second_ref[0, part], h[...]) + nt(second_ref[0, part], l[...])
             + nt(second_ref[1, part], h[...]))
        spec_ref[part] = s
        re, im = s[:HALF], s[HALF:]
        feature = jnp.log1p((re * re + im * im) * (1.0 / SEQ))
        for c in range(per):
            for k in range(STEP):
                feat_ref[pl.ds(part * count * stride + STEP * c + k, count, stride=stride), :] = (
                    feature[count * k : count * (k + 1), HALF * c : HALF * (c + 1)])


def reduce_kernel(per, hid, f_ref, out_ref):
    stride = 2 * TILE
    pieces = f_ref.shape[0] // stride

    def rows(r):
        return f_ref[pl.ds(r, pieces, stride=stride), :]

    weights = [rows(TILE + c) for c in range(per)]
    left = jnp.concatenate([w.T[:hid] for w in weights], 1).astype(bf16)
    features = jnp.concatenate(
        [jnp.concatenate([rows(STEP * c + k) for c in range(per)], 0) for k in range(STEP)], 1)
    high, low = split(features)
    pre = mm(left, jnp.concatenate([high, low], 1))
    width = STEP * HALF
    out_ref[:hid] = (pre[:, :width] + pre[:, width:]) * (1.0 / IN_SCALE)
    last = rows(TILE + per)
    extra = weights[0] * last[:, 0:1]
    for c in range(1, per):
        extra = extra + weights[c] * last[:, c : c + 1]
    extra = jnp.sum(extra, axis=0, keepdims=True) * (1.0 / IN_SCALE)
    out_ref[hid:, :128] = jnp.broadcast_to(extra, (TILE, 128))
    out_ref[hid:, 128:] = jnp.zeros((TILE, width - 128), f32)


def gelu(v):
    return 0.5 * v * (1.0 + lax.erf(v * math.sqrt(0.5)))


def gain_kernel(per, hid, r_ref, f_ref, bias_ref, cout_ref, out_ref, gain_ref):
    total = r_ref[0]
    for g in range(1, r_ref.shape[0]):
        total = total + r_ref[g]
    bias = bias_ref[0:1]
    column = jnp.sum(jnp.where(iota((hid, hid), 1) == iota((hid, hid), 0), bias, 0.0),
                     axis=1, keepdims=True)
    high, low = split(gelu(total[:hid] + column))
    hidden = jnp.concatenate([high, low], 1)
    hidden = jnp.concatenate([jnp.zeros_like(hidden), hidden], 0)
    stride = 2 * TILE
    pieces = f_ref.shape[0] // stride
    width = STEP * HALF
    for c in range(per):
        weights = f_ref[pl.ds(TILE + c, pieces, stride=stride), :].astype(bf16)
        g = mm(weights, hidden)
        g = (g[:, :width] + g[:, width:]) * (GAIN_SCALE / OUT_SCALE)
        for k in range(STEP):
            out_ref[pl.ds(STEP * c + k, pieces, stride=TILE), :] = g[:, HALF * k : HALF * (k + 1)]
    high, low = split(gelu(total[hid:, :hid] + bias))
    gain_ref[...] = mm(high, cout_ref[...]) + mm(low, cout_ref[...])


def inverse_kernel(per, block, g_ref, spec_ref, nyq_ref, gain_ref, skip_ref, r_ref,
                   inv_ref, twf_ref, last_ref, row0_ref, out_ref):
    members = r_ref.shape[0]
    width = HALF * per
    count = HALF // STEP
    sums = []
    for part in range(2):
        g = jnp.concatenate([
            jnp.concatenate([
                g_ref[pl.ds(part * count * TILE + STEP * c + k, count, stride=TILE), :]
                for k in range(STEP)], 0)
            for c in range(per)], 1) * (1.0 / GAIN_SCALE)
        if part == 0:
            dc = (iota((HALF, width), 0) == 0) & (iota((HALF, width), 1) % HALF == 0)
            g = jnp.where(dc, 0.5 * g, g)
        s = spec_ref[part]
        high, low = split(jnp.concatenate([s[:HALF] * g, s[HALF:] * g], 0))
        sums.append(mm(inv_ref[0, part], high) + mm(inv_ref[0, part], low)
                    + mm(inv_ref[1, part], high))
    own = first_channel(per)
    lane = iota((1, 128), 1)
    cosine, sine = twf_ref[0].T, twf_ref[1].T
    shared_cos, shared_sin = row0_ref[0].T[:, 0:1], row0_ref[1].T[:, 0:1]
    lane0 = iota((RADIX, HALF), 1) == 0
    outs = []
    for c in range(per):
        cols = slice(HALF * c, HALF * (c + 1))
        top_re, top_im = sums[0][:RADIX, cols], sums[0][RADIX:, cols]
        bot_re, bot_im = sums[1][:RADIX, cols], sums[1][RADIX:, cols]
        re = jnp.where(lane0, top_re, top_re + bot_re)
        im = top_im + bot_im
        out_re = jnp.where(lane0, re, re * cosine - im * sine)
        out_im = jnp.where(lane0, bot_re * shared_cos - bot_im * shared_sin,
                           re * sine + im * cosine)
        high, low = split(jnp.concatenate([out_re, out_im], 1))
        y = nt(last_ref[0], high) + nt(last_ref[0], low) + nt(last_ref[1], high)
        mine = lane == own + c
        skip = jnp.sum(jnp.where(mine, skip_ref[0:1], 0.0), axis=1, keepdims=True)
        gain = jnp.sum(jnp.where(mine, gain_ref[0:1], 0.0), axis=1, keepdims=True)
        spare = jnp.sum(jnp.where(lane == c, nyq_ref[0:1], 0.0), axis=1, keepdims=True)
        x = r_ref[:, block * c : block * (c + 1), :].astype(f32).reshape(RADIX, RADIX)
        y = y + (spare * gain * (1.0 / SEQ)) * row0_ref[2, 0:1] + skip * x
        outs.append(y.reshape(members, block, RADIX))
    out_ref[...] = jnp.concatenate(outs, 1).astype(bf16)


def call(kernel, outs, scratch=(), source=pltpu.VMEM, target=pltpu.VMEM):
    many = isinstance(outs, (list, tuple))

    def run(*args):
        return pl.pallas_call(
            kernel,
            out_shape=outs,
            in_specs=[pl.BlockSpec(memory_space=source)] * len(args),
            out_specs=[pl.BlockSpec(memory_space=target)] * len(outs) if many
            else pl.BlockSpec(memory_space=target),
            scratch_shapes=list(scratch),
            compiler_params=pltpu.CompilerParams(vmem_limit_bytes=40 * 1024 * 1024),
        )(*args)

    return run


def exchange(x, axis):
    return lax.all_to_all(x, axis, split_axis=0, concat_axis=0, tiled=True)


def on_device(signal, cond_in, cond_bias, cond_out, skip_gain):
    shape = jax.ShapeDtypeStruct
    ctx, spread, line = ("y", "xh", "core"), ("y", "z", "core"), ("xl", "xh")
    members = lax.axis_size(ctx)
    pieces = lax.axis_size(spread)
    groups = lax.axis_size(line)
    seq_local, chan = signal.shape
    hid = cond_in.shape[1]
    per = chan // members
    block = seq_local // RADIX
    width = HALF * per
    t = tables(tuple(lax.axis_size(name) for name in ("xh", "y", "core")))
    t = {name: jnp.asarray(value) for name, value in t.items()}
    buffers = [pltpu.VMEM((chan * block, 128), f32)] * 2 + [
        pltpu.VMEM((seq_local, chan), bf16), pltpu.SemaphoreType.DMA((block + 2,))]
    piece = shape((members, per * block, RADIX), bf16)

    def send(x, axis, count):
        x = x.astype(f16).reshape(count, -1, x.shape[-1])
        return exchange(x, axis).astype(f32)

    packed, bias, skip = call(
        pack_kernel, [piece, shape((1, hid), f32), shape((1, chan), f32)], buffers,
        source=pltpu.HBM)(signal, cond_bias.reshape(1, hid), skip_gain.reshape(1, chan))
    received = exchange(packed, ctx)
    feat, spec, nyq, last, cout = call(
        functools.partial(forward_kernel, per, block),
        [shape((pieces * 2 * TILE, HALF), f32), shape((2, RADIX, width), f32),
         shape((8, 128), f32), shape((2, RADIX, RADIX), bf16), shape((hid, chan), bf16)],
        [pltpu.VMEM((width, 2 * RADIX), bf16)] * 4)(
            received, t["first"], t["twf"], t["row0"], t["second"], t["last"],
            cond_in.T, cond_out)
    feat = send(feat, spread, pieces).reshape(feat.shape)
    partial = call(functools.partial(reduce_kernel, per, hid),
                   shape((hid + TILE, STEP * HALF), f32))(feat)
    partial = jnp.broadcast_to(partial[None], (groups,) + partial.shape)
    partial = send(partial, line, groups)
    gain, spare_gain = call(functools.partial(gain_kernel, per, hid),
                            [shape((pieces * TILE, HALF), f32), shape((8, chan), f32)])(
                                partial, feat, bias, cout)
    gain = send(gain, spread, pieces).reshape(gain.shape)
    mixed = call(functools.partial(inverse_kernel, per, block), piece)(
        gain, spec, nyq, spare_gain, skip, received, t["inv"], t["twf"], last, t["row0"])
    mixed = exchange(mixed, ctx)
    return call(unpack_kernel, shape((seq_local, chan), bf16), buffers,
                target=pltpu.HBM)(mixed)


def solution(mesh):
    fine = Mesh(mesh.devices.reshape(2, -1, 2, 2, mesh.devices.shape[1] // 2),
                ("xh", "y", "core", "xl", "z"))
    ctx, ch = ("xh", "y", "core"), ("xl", "z")
    return jax.shard_map(
        on_device,
        mesh=fine,
        in_specs=(P(ctx, ch), P(ch, None), P(), P(None, ch), P(ch)),
        out_specs=P(ctx, ch),
        check_vma=False,
    )
```

```python
import functools
import math

import jax
import jax.numpy as jnp
import numpy as np
from jax import lax
from jax.experimental import pallas as pl
from jax.experimental.pallas import tpu as pltpu
from jax.sharding import Mesh
from jax.sharding import PartitionSpec as P

f32, bf16, f16 = jnp.float32, jnp.bfloat16, jnp.float16

RADIX = 256
HALF = RADIX // 2
SEQ = RADIX * RADIX
STEP = 2
TILE = 8
GAIN_SCALE = 0.25
IN_SCALE = 2.0**18
OUT_SCALE = 2.0**16


def split_const(values):
    high = values.astype(np.float32).astype(jnp.bfloat16)
    low = (values - high.astype(np.float64)).astype(np.float32).astype(jnp.bfloat16)
    return high, low


@functools.lru_cache(maxsize=None)
def tables(sizes):
    arrival = np.arange(math.prod(sizes)).reshape(sizes).transpose(1, 0, 2).reshape(-1)
    block = RADIX // arrival.size
    position = (arrival[:, None] * block + np.arange(block)).reshape(-1)
    n = np.arange(RADIX, dtype=np.float64)
    k = np.arange(HALF, dtype=np.float64)
    tau = 2.0 * np.pi
    angle = tau * np.outer(k, n) / RADIX
    first = np.concatenate([np.cos(angle), -np.sin(angle)], 0)
    first[HALF] = np.cos(math.pi * n)
    first = np.concatenate(split_const(first[:, position]), 0)
    angle = tau * np.outer(k, n) / SEQ
    cos_f, sin_f = np.cos(angle), np.sin(angle)
    cos_g = cos_f.copy()
    cos_g[0] = 0.0
    shared = tau * n * (HALF + SEQ // 2) / SEQ
    twf = np.stack([cos_f, sin_f, cos_g]).astype(np.float32)
    row0 = np.zeros((3, 8, RADIX))
    row0[0, 0], row0[1, 0] = np.cos(shared), np.sin(shared)
    row0[2, :] = np.cos(math.pi * n)
    row0 = row0.astype(np.float32)
    angle = tau * np.outer(n, n) / RADIX
    wre, wim = np.cos(angle), -np.sin(angle)
    full = [np.concatenate([wre, -wim], 1), np.concatenate([wim, wre], 1)]
    order = np.arange(HALF).reshape(-1, STEP).T.reshape(-1)
    second = np.stack([np.concatenate([f[order] for f in full], 0),
                       np.concatenate([f[HALF + order] for f in full], 0)])
    second = np.stack(split_const(second))
    vre, vim = np.cos(angle), np.sin(angle)
    inv = np.stack([
        np.concatenate([np.concatenate([vre[:, s], -vim[:, s]], 1),
                        np.concatenate([vim[:, s], vre[:, s]], 1)], 0)
        for s in (order, HALF + order)])
    inv = np.stack(split_const(inv))
    angle = tau * np.outer(n, k) / RADIX
    last = np.concatenate([np.cos(angle), -np.sin(angle)], 1)
    last[:, HALF] = np.cos(math.pi * n)
    last = np.stack(split_const(last[position] * (2.0 / SEQ)))
    return dict(first=first, twf=twf, row0=row0, second=second, inv=inv, last=last)


def split(x):
    high = x.astype(bf16)
    return high, (x - high.astype(f32)).astype(bf16)


def mm(a, b):
    return jnp.dot(a, b, preferred_element_type=f32)


def nt(a, b):
    return lax.dot_general(a, b, (((1,), (1,)), ((), ())), preferred_element_type=f32)


def iota(shape, axis):
    return lax.broadcasted_iota(jnp.int32, shape, axis)


def first_channel(per):
    index = lax.axis_index("y") * lax.axis_size("xh") + lax.axis_index("xh")
    return (index * lax.axis_size("core") + lax.axis_index("core")) * per


def pack_kernel(x_ref, out_ref, left, right):
    rows = x_ref.shape[0] // RADIX
    chan = x_ref.shape[1]
    for a in range(rows):
        block = x_ref[RADIX * a : RADIX * (a + 1), :].astype(f32).T
        left[pl.ds(a, chan, stride=rows), :] = block[:, :128]
        right[pl.ds(a, chan, stride=rows), :] = block[:, 128:]
    out_ref[:, :, :128] = left[...].astype(bf16).reshape(out_ref.shape[:2] + (128,))
    out_ref[:, :, 128:] = right[...].astype(bf16).reshape(out_ref.shape[:2] + (128,))


def unpack_kernel(r_ref, out_ref, left, right):
    rows = out_ref.shape[0] // RADIX
    chan = out_ref.shape[1]
    left[...] = r_ref[:, :, :128].astype(f32).reshape(left.shape)
    right[...] = r_ref[:, :, 128:].astype(f32).reshape(right.shape)
    for a in range(rows):
        out_ref[RADIX * a : RADIX * a + 128, :] = (
            left[pl.ds(a, chan, stride=rows), :].T.astype(bf16))
        out_ref[RADIX * a + 128 : RADIX * (a + 1), :] = (
            right[pl.ds(a, chan, stride=rows), :].T.astype(bf16))


def forward_kernel(per, block, r_ref, first_ref, twf_ref, row0_ref, second_ref, last_in_ref,
                   cin_ref, cout_in_ref, bias_in_ref, skip_in_ref,
                   feat_ref, spec_ref, nyq_ref, last_ref, cout_ref, bias_ref, skip_ref,
                   hi, lo, hi2, lo2):
    last_ref[...] = last_in_ref[...]
    cout_ref[...] = cout_in_ref[...]
    bias_ref[...] = jnp.broadcast_to(bias_in_ref[...], bias_ref.shape)
    skip_ref[...] = jnp.broadcast_to(skip_in_ref[...], skip_ref.shape)
    values = r_ref[...].astype(f32)
    first_row = iota((8, RADIX), 0) == 0
    spare = jnp.zeros((8, 128), f32)
    spare_lane = iota((8, 128), 1)
    for c in range(per):
        x = values[:, block * c : block * (c + 1), :].reshape(RADIX, RADIX).astype(bf16)
        a = mm(first_ref[...], x)
        a = a[:RADIX] + a[RADIX:]
        re, im = a[:HALF], a[HALF:]
        out_re = re * twf_ref[0] + im * twf_ref[1]
        out_im = im * twf_ref[2] - re * twf_ref[1]
        place = pl.ds(HALF * c, HALF)
        for at, part in ((0, out_re), (RADIX, out_im)):
            high, low = split(part)
            hi[place, at : at + RADIX], lo[place, at : at + RADIX] = high, low
            hi2[place, at : at + RADIX], lo2[place, at : at + RADIX] = high, low
        lead = im[0:8]
        top = pl.ds(HALF * c, 16)
        alt_re = jnp.concatenate(
            [jnp.where(first_row, lead * row0_ref[0], out_re[0:8]), out_re[8:16]], 0)
        alt_im = jnp.concatenate(
            [jnp.where(first_row, -lead * row0_ref[1], out_im[0:8]), out_im[8:16]], 0)
        for at, part in ((0, alt_re), (RADIX, alt_im)):
            high, low = split(part)
            hi2[top, at : at + RADIX], lo2[top, at : at + RADIX] = high, low
        nyq = jnp.sum(re[0:1] * row0_ref[2, 0:1], axis=1, keepdims=True)
        spare = jnp.where(spare_lane == c, nyq, spare)
    nyq_ref[...] = spare
    chan = cin_ref.shape[1]
    row = iota((TILE, chan), 0)
    select = ((iota((TILE, chan), 1) == first_channel(per) + row) & (row < per))
    select = select.astype(f32).astype(bf16)
    tile = jnp.concatenate([nt(select, cin_ref[...]) * IN_SCALE,
                            nt(select, cout_in_ref[...]) * OUT_SCALE], 1)
    tile = jnp.where(iota((TILE, 128), 0) == per, jnp.log1p(spare * spare * (1.0 / SEQ)), tile)
    stride = 2 * TILE
    pieces = feat_ref.shape[0] // stride
    for r in range(TILE):
        feat_ref[pl.ds(TILE + r, pieces, stride=stride), :] = jnp.broadcast_to(
            tile[r : r + 1], (pieces, 128))
    count = HALF // STEP
    for part, (h, l) in enumerate(((hi, lo), (hi2, lo2))):
        s = (nt(second_ref[0, part], h[...]) + nt(second_ref[0, part], l[...])
             + nt(second_ref[1, part], h[...]))
        spec_ref[part] = s
        re, im = s[:HALF], s[HALF:]
        feature = jnp.log1p((re * re + im * im) * (1.0 / SEQ))
        for c in range(per):
            for k in range(STEP):
                feat_ref[pl.ds(part * count * stride + STEP * c + k, count, stride=stride), :] = (
                    feature[count * k : count * (k + 1), HALF * c : HALF * (c + 1)])


def reduce_kernel(per, hid, f_ref, out_ref):
    stride = 2 * TILE
    pieces = f_ref.shape[0] // stride

    def rows(r):
        return f_ref[pl.ds(r, pieces, stride=stride), :]

    weights = [rows(TILE + c) for c in range(per)]
    left = jnp.concatenate([w.T[:hid] for w in weights], 1).astype(bf16)
    features = jnp.concatenate(
        [jnp.concatenate([rows(STEP * c + k) for c in range(per)], 0) for k in range(STEP)], 1)
    high, low = split(features)
    pre = mm(left, jnp.concatenate([high, low], 1))
    width = STEP * HALF
    out_ref[:hid] = (pre[:, :width] + pre[:, width:]) * (1.0 / IN_SCALE)
    last = rows(TILE + per)
    extra = weights[0] * last[:, 0:1]
    for c in range(1, per):
        extra = extra + weights[c] * last[:, c : c + 1]
    extra = jnp.sum(extra, axis=0, keepdims=True) * (1.0 / IN_SCALE)
    out_ref[hid:, :128] = jnp.broadcast_to(extra, (TILE, 128))
    out_ref[hid:, 128:] = jnp.zeros((TILE, width - 128), f32)


def gelu(v):
    return 0.5 * v * (1.0 + lax.erf(v * math.sqrt(0.5)))


def gain_kernel(per, hid, r_ref, f_ref, bias_ref, cout_ref, out_ref, gain_ref):
    total = r_ref[0]
    for g in range(1, r_ref.shape[0]):
        total = total + r_ref[g]
    bias = bias_ref[0:1]
    column = jnp.sum(jnp.where(iota((hid, hid), 1) == iota((hid, hid), 0), bias, 0.0),
                     axis=1, keepdims=True)
    high, low = split(gelu(total[:hid] + column))
    hidden = jnp.concatenate([high, low], 1)
    hidden = jnp.concatenate([jnp.zeros_like(hidden), hidden], 0)
    stride = 2 * TILE
    pieces = f_ref.shape[0] // stride
    width = STEP * HALF
    for c in range(per):
        weights = f_ref[pl.ds(TILE + c, pieces, stride=stride), :].astype(bf16)
        g = mm(weights, hidden)
        g = (g[:, :width] + g[:, width:]) * (GAIN_SCALE / OUT_SCALE)
        for k in range(STEP):
            out_ref[pl.ds(STEP * c + k, pieces, stride=TILE), :] = g[:, HALF * k : HALF * (k + 1)]
    high, low = split(gelu(total[hid:, :hid] + bias))
    gain_ref[...] = mm(high, cout_ref[...]) + mm(low, cout_ref[...])


def inverse_kernel(per, block, g_ref, spec_ref, nyq_ref, gain_ref, skip_ref, r_ref,
                   inv_ref, twf_ref, last_ref, row0_ref, out_ref):
    members = r_ref.shape[0]
    width = HALF * per
    count = HALF // STEP
    sums = []
    for part in range(2):
        g = jnp.concatenate([
            jnp.concatenate([
                g_ref[pl.ds(part * count * TILE + STEP * c + k, count, stride=TILE), :]
                for k in range(STEP)], 0)
            for c in range(per)], 1) * (1.0 / GAIN_SCALE)
        if part == 0:
            dc = (iota((HALF, width), 0) == 0) & (iota((HALF, width), 1) % HALF == 0)
            g = jnp.where(dc, 0.5 * g, g)
        s = spec_ref[part]
        high, low = split(jnp.concatenate([s[:HALF] * g, s[HALF:] * g], 0))
        sums.append(mm(inv_ref[0, part], high) + mm(inv_ref[0, part], low)
                    + mm(inv_ref[1, part], high))
    own = first_channel(per)
    lane = iota((1, 128), 1)
    cosine, sine = twf_ref[0].T, twf_ref[1].T
    shared_cos, shared_sin = row0_ref[0].T[:, 0:1], row0_ref[1].T[:, 0:1]
    lane0 = iota((RADIX, HALF), 1) == 0
    outs = []
    for c in range(per):
        cols = slice(HALF * c, HALF * (c + 1))
        top_re, top_im = sums[0][:RADIX, cols], sums[0][RADIX:, cols]
        bot_re, bot_im = sums[1][:RADIX, cols], sums[1][RADIX:, cols]
        re = jnp.where(lane0, top_re, top_re + bot_re)
        im = top_im + bot_im
        out_re = jnp.where(lane0, re, re * cosine - im * sine)
        out_im = jnp.where(lane0, bot_re * shared_cos - bot_im * shared_sin,
                           re * sine + im * cosine)
        high, low = split(jnp.concatenate([out_re, out_im], 1))
        y = nt(last_ref[0], high) + nt(last_ref[0], low) + nt(last_ref[1], high)
        mine = lane == own + c
        skip = jnp.sum(jnp.where(mine, skip_ref[0:1], 0.0), axis=1, keepdims=True)
        gain = jnp.sum(jnp.where(mine, gain_ref[0:1], 0.0), axis=1, keepdims=True)
        spare = jnp.sum(jnp.where(lane == c, nyq_ref[0:1], 0.0), axis=1, keepdims=True)
        x = r_ref[:, block * c : block * (c + 1), :].astype(f32).reshape(RADIX, RADIX)
        y = y + (spare * gain * (1.0 / SEQ)) * row0_ref[2, 0:1] + skip * x
        outs.append(y.reshape(members, block, RADIX))
    out_ref[...] = jnp.concatenate(outs, 1).astype(bf16)


def call(kernel, outs, scratch=(), flops=0, interpret=False):
    vmem = pl.BlockSpec(memory_space=pltpu.VMEM)
    many = isinstance(outs, (list, tuple))

    def run(*args):
        return pl.pallas_call(
            kernel,
            out_shape=outs,
            in_specs=[vmem] * len(args),
            out_specs=[vmem] * len(outs) if many else vmem,
            scratch_shapes=list(scratch),
            compiler_params=pltpu.CompilerParams(vmem_limit_bytes=40 * 1024 * 1024),
        )(*args)

    return run


def exchange(x, axis):
    return lax.all_to_all(x, axis, split_axis=0, concat_axis=0, tiled=True)


def on_device(signal, cond_in, cond_bias, cond_out, skip_gain):
    shape = jax.ShapeDtypeStruct
    ctx, spread, line = ("y", "xh", "core"), ("y", "z", "core"), ("xl", "xh")
    members = lax.axis_size(ctx)
    pieces = lax.axis_size(spread)
    groups = lax.axis_size(line)
    seq_local, chan = signal.shape
    hid = cond_in.shape[1]
    per = chan // members
    block = seq_local // RADIX
    width = HALF * per
    t = tables(tuple(lax.axis_size(name) for name in ("xh", "y", "core")))
    t = {name: jnp.asarray(value) for name, value in t.items()}
    halves = [pltpu.VMEM((chan * block, 128), f32)] * 2
    piece = shape((members, per * block, RADIX), bf16)

    def send(x, axis, count):
        x = x.astype(f16).reshape(count, -1, x.shape[-1])
        return exchange(x, axis).astype(f32)

    packed = call(pack_kernel, piece, halves)(signal)
    received = exchange(packed, ctx)
    feat, spec, nyq, last, cout, bias, skip = call(
        functools.partial(forward_kernel, per, block),
        [shape((pieces * 2 * TILE, HALF), f32), shape((2, RADIX, width), f32),
         shape((8, 128), f32), shape((2, RADIX, RADIX), bf16), shape((hid, chan), bf16),
         shape((8, hid), f32), shape((8, chan), f32)],
        [pltpu.VMEM((width, 2 * RADIX), bf16)] * 4)(
            received, t["first"], t["twf"], t["row0"], t["second"], t["last"],
            cond_in.T, cond_out, cond_bias.reshape(1, hid), skip_gain.reshape(1, chan))
    feat = send(feat, spread, pieces).reshape(feat.shape)
    partial = call(functools.partial(reduce_kernel, per, hid),
                   shape((hid + TILE, STEP * HALF), f32))(feat)
    partial = jnp.broadcast_to(partial[None], (groups,) + partial.shape)
    partial = send(partial, line, groups)
    gain, spare_gain = call(functools.partial(gain_kernel, per, hid),
                            [shape((pieces * TILE, HALF), f32), shape((8, chan), f32)])(
                                partial, feat, bias, cout)
    gain = send(gain, spread, pieces).reshape(gain.shape)
    mixed = call(functools.partial(inverse_kernel, per, block), piece)(
        gain, spec, nyq, spare_gain, skip, received, t["inv"], t["twf"], last, t["row0"])
    mixed = exchange(mixed, ctx)
    return call(unpack_kernel, shape((seq_local, chan), bf16), halves)(mixed)


def solution(mesh):
    fine = Mesh(mesh.devices.reshape(2, -1, 2, 2, mesh.devices.shape[1] // 2),
                ("xh", "y", "core", "xl", "z"))
    ctx, ch = ("xh", "y", "core"), ("xl", "z")
    return jax.shard_map(
        on_device,
        mesh=fine,
        in_specs=(P(ctx, ch), P(ch, None), P(), P(None, ch), P(ch)),
        out_specs=P(ctx, ch),
        check_vma=False,
    )
```

```python
import functools
import math

import jax
import jax.numpy as jnp
import numpy as np
from jax import lax
from jax.experimental import pallas as pl
from jax.experimental.pallas import tpu as pltpu
from jax.sharding import Mesh
from jax.sharding import PartitionSpec as P

f32, bf16, f16 = jnp.float32, jnp.bfloat16, jnp.float16

RADIX = 256
HALF = RADIX // 2
SEQ = RADIX * RADIX
STEP = 2
TILE, REST = 8, 6
GAIN_SCALE = 0.25
IN_SCALE = 2.0**18
OUT_SCALE = 2.0**16


def split_const(values):
    high = values.astype(np.float32).astype(jnp.bfloat16)
    low = (values - high.astype(np.float64)).astype(np.float32).astype(jnp.bfloat16)
    return high, low


@functools.lru_cache(maxsize=None)
def tables(sizes):
    arrival = np.arange(math.prod(sizes)).reshape(sizes).transpose(1, 0, 2).reshape(-1)
    block = RADIX // arrival.size
    position = (arrival[:, None] * block + np.arange(block)).reshape(-1)
    n = np.arange(RADIX, dtype=np.float64)
    k = np.arange(HALF, dtype=np.float64)
    tau = 2.0 * np.pi
    angle = tau * np.outer(k, n) / RADIX
    first = np.concatenate([np.cos(angle), -np.sin(angle)], 0)
    first[HALF] = np.cos(math.pi * n)
    first = np.concatenate(split_const(first[:, position]), 0)
    angle = tau * np.outer(k, n) / SEQ
    cos_f, sin_f = np.cos(angle), np.sin(angle)
    cos_g = cos_f.copy()
    cos_g[0] = 0.0
    shared = tau * n * (HALF + SEQ // 2) / SEQ
    twf = np.stack([cos_f, sin_f, cos_g]).astype(np.float32)
    row0 = np.zeros((3, 8, RADIX))
    row0[0, 0], row0[1, 0] = np.cos(shared), np.sin(shared)
    row0[2, :] = np.cos(math.pi * n)
    twf = np.concatenate([twf, row0.astype(np.float32)], 1)
    angle = tau * np.outer(n, n) / RADIX
    wre, wim = np.cos(angle), -np.sin(angle)
    full = [np.concatenate([wre, -wim], 1), np.concatenate([wim, wre], 1)]
    order = np.arange(HALF).reshape(-1, STEP).T.reshape(-1)
    second = np.stack([np.concatenate([f[order] for f in full], 0),
                       np.concatenate([f[HALF + order] for f in full], 0)])
    second = np.stack(split_const(second))
    vre, vim = np.cos(angle), np.sin(angle)
    inv = np.stack([
        np.concatenate([np.concatenate([vre[:, s], -vim[:, s]], 1),
                        np.concatenate([vim[:, s], vre[:, s]], 1)], 0)
        for s in (order, HALF + order)])
    inv = np.stack(split_const(inv))
    angle = tau * np.outer(n, k) / RADIX
    last = np.concatenate([np.cos(angle), -np.sin(angle)], 1)
    last[:, HALF] = np.cos(math.pi * n)
    last = np.concatenate(split_const(last[position] * (2.0 / SEQ)), 0)
    ends = np.stack([first, last])
    return dict(ends=ends, twf=twf, second=second, inv=inv)


def split(x):
    high = x.astype(bf16)
    return high, (x - high.astype(f32)).astype(bf16)


def mm(a, b):
    return jnp.dot(a, b, preferred_element_type=f32)


def nt(a, b):
    return lax.dot_general(a, b, (((1,), (1,)), ((), ())), preferred_element_type=f32)


def iota(shape, axis):
    return lax.broadcasted_iota(jnp.int32, shape, axis)


def first_channel(per):
    index = lax.axis_index("y") * lax.axis_size("xh") + lax.axis_index("xh")
    return (index * lax.axis_size("core") + lax.axis_index("core")) * per


def pack_kernel(x_ref, out_ref, left, right):
    rows = x_ref.shape[0] // RADIX
    chan = x_ref.shape[1]
    for a in range(rows):
        block = x_ref[RADIX * a : RADIX * (a + 1), :].astype(f32).T
        left[pl.ds(a, chan, stride=rows), :] = block[:, :128]
        right[pl.ds(a, chan, stride=rows), :] = block[:, 128:]
    out_ref[:, :, :128] = left[...].astype(bf16).reshape(out_ref.shape[:2] + (128,))
    out_ref[:, :, 128:] = right[...].astype(bf16).reshape(out_ref.shape[:2] + (128,))


def unpack_kernel(r_ref, out_ref, left, right):
    rows = out_ref.shape[0] // RADIX
    chan = out_ref.shape[1]
    left[...] = r_ref[:, :, :128].astype(f32).reshape(left.shape)
    right[...] = r_ref[:, :, 128:].astype(f32).reshape(right.shape)
    for a in range(rows):
        out_ref[RADIX * a : RADIX * a + 128, :] = (
            left[pl.ds(a, chan, stride=rows), :].T.astype(bf16))
        out_ref[RADIX * a + 128 : RADIX * (a + 1), :] = (
            right[pl.ds(a, chan, stride=rows), :].T.astype(bf16))


def forward_kernel(per, block, r_ref, ends_ref, twf_ref, second_ref,
                   cin_ref, cout_in_ref, bias_in_ref, skip_in_ref,
                   feat_ref, spec_ref, nyq_ref, cout_ref, bias_ref, skip_ref,
                   hi, lo, hi2, lo2):
    cout_ref[...] = cout_in_ref[...]
    bias_ref[...] = jnp.broadcast_to(bias_in_ref[...], bias_ref.shape)
    skip_ref[...] = jnp.broadcast_to(skip_in_ref[...], skip_ref.shape)
    values = r_ref[...].astype(f32)
    first_row = iota((8, RADIX), 0) == 0
    spare = jnp.zeros((8, 128), f32)
    spare_lane = iota((8, 128), 1)
    for c in range(per):
        x = values[:, block * c : block * (c + 1), :].reshape(RADIX, RADIX).astype(bf16)
        a = mm(ends_ref[0], x)
        a = a[:RADIX] + a[RADIX:]
        re, im = a[:HALF], a[HALF:]
        out_re = re * twf_ref[0, :HALF] + im * twf_ref[1, :HALF]
        out_im = im * twf_ref[2, :HALF] - re * twf_ref[1, :HALF]
        place = pl.ds(HALF * c, HALF)
        for at, part in ((0, out_re), (RADIX, out_im)):
            high, low = split(part)
            hi[place, at : at + RADIX], lo[place, at : at + RADIX] = high, low
            hi2[place, at : at + RADIX], lo2[place, at : at + RADIX] = high, low
        lead = im[0:8]
        top = pl.ds(HALF * c, 16)
        alt_re = jnp.concatenate(
            [jnp.where(first_row, lead * twf_ref[0, HALF:], out_re[0:8]), out_re[8:16]], 0)
        alt_im = jnp.concatenate(
            [jnp.where(first_row, -lead * twf_ref[1, HALF:], out_im[0:8]), out_im[8:16]], 0)
        for at, part in ((0, alt_re), (RADIX, alt_im)):
            high, low = split(part)
            hi2[top, at : at + RADIX], lo2[top, at : at + RADIX] = high, low
        nyq = jnp.sum(re[0:1] * twf_ref[2, HALF : HALF + 1], axis=1, keepdims=True)
        spare = jnp.where(spare_lane == c, nyq, spare)
    nyq_ref[...] = spare
    chan = cin_ref.shape[1]
    row = iota((TILE, chan), 0)
    select = ((iota((TILE, chan), 1) == first_channel(per) + row) & (row < per))
    select = select.astype(f32).astype(bf16)
    tile = jnp.concatenate([nt(select, cin_ref[...]) * IN_SCALE,
                            nt(select, cout_in_ref[...]) * OUT_SCALE], 1)
    tile = jnp.where(iota((TILE, 128), 0) == per, jnp.log1p(spare * spare * (1.0 / SEQ)), tile)
    stride = TILE + REST
    pieces = feat_ref.shape[0] // stride
    for r in range(REST):
        feat_ref[pl.ds(TILE + r, pieces, stride=stride), :] = jnp.broadcast_to(
            tile[r : r + 1], (pieces, 128))
    count = HALF // STEP
    for part, (h, l) in enumerate(((hi, lo), (hi2, lo2))):
        s = (nt(second_ref[0, part], h[...]) + nt(second_ref[0, part], l[...])
             + nt(second_ref[1, part], h[...]))
        spec_ref[part] = s
        re, im = s[:HALF], s[HALF:]
        feature = jnp.log1p((re * re + im * im) * (1.0 / SEQ))
        for c in range(per):
            for k in range(STEP):
                feat_ref[pl.ds(part * count * stride + STEP * c + k, count, stride=stride), :] = (
                    feature[count * k : count * (k + 1), HALF * c : HALF * (c + 1)])


def reduce_kernel(per, hid, f_ref, out_ref):
    stride = TILE + REST
    pieces = f_ref.shape[0] // stride

    def rows(r):
        return f_ref[pl.ds(r, pieces, stride=stride), :]

    weights = [rows(TILE + c) for c in range(per)]
    left = jnp.concatenate([w.T[:hid] for w in weights], 1).astype(bf16)
    features = jnp.concatenate(
        [jnp.concatenate([rows(STEP * c + k) for c in range(per)], 0) for k in range(STEP)], 1)
    high, low = split(features)
    pre = mm(left, jnp.concatenate([high, low], 1))
    width = STEP * HALF
    out_ref[:hid] = (pre[:, :width] + pre[:, width:]) * (1.0 / IN_SCALE)
    last = rows(TILE + per)
    extra = weights[0] * last[:, 0:1]
    for c in range(1, per):
        extra = extra + weights[c] * last[:, c : c + 1]
    extra = jnp.sum(extra, axis=0, keepdims=True) * (1.0 / IN_SCALE)
    out_ref[hid:, :128] = jnp.broadcast_to(extra, (TILE, 128))
    out_ref[hid:, 128:] = jnp.zeros((TILE, width - 128), f32)


def gelu(v):
    return 0.5 * v * (1.0 + lax.erf(v * math.sqrt(0.5)))


def gain_kernel(per, hid, r_ref, f_ref, bias_ref, cout_ref, out_ref, gain_ref):
    total = r_ref[0]
    for g in range(1, r_ref.shape[0]):
        total = total + r_ref[g]
    bias = bias_ref[0:1]
    column = jnp.sum(jnp.where(iota((hid, hid), 1) == iota((hid, hid), 0), bias, 0.0),
                     axis=1, keepdims=True)
    high, low = split(gelu(total[:hid] + column))
    hidden = jnp.concatenate([high, low], 1)
    hidden = jnp.concatenate([jnp.zeros_like(hidden), hidden], 0)
    stride = TILE + REST
    pieces = f_ref.shape[0] // stride
    width = STEP * HALF
    for c in range(per):
        weights = f_ref[pl.ds(TILE + c, pieces, stride=stride), :].astype(bf16)
        g = mm(weights, hidden)
        g = (g[:, :width] + g[:, width:]) * (GAIN_SCALE / OUT_SCALE)
        for k in range(STEP):
            out_ref[pl.ds(STEP * c + k, pieces, stride=TILE), :] = g[:, HALF * k : HALF * (k + 1)]
    high, low = split(gelu(total[hid:, :hid] + bias))
    gain_ref[...] = mm(high, cout_ref[...]) + mm(low, cout_ref[...])


def inverse_kernel(per, block, g_ref, spec_ref, nyq_ref, gain_ref, skip_ref, r_ref,
                   inv_ref, twf_ref, ends_ref, out_ref):
    members = r_ref.shape[0]
    width = HALF * per
    count = HALF // STEP
    sums = []
    for part in range(2):
        g = jnp.concatenate([
            jnp.concatenate([
                g_ref[pl.ds(part * count * TILE + STEP * c + k, count, stride=TILE), :]
                for k in range(STEP)], 0)
            for c in range(per)], 1) * (1.0 / GAIN_SCALE)
        if part == 0:
            dc = (iota((HALF, width), 0) == 0) & (iota((HALF, width), 1) % HALF == 0)
            g = jnp.where(dc, 0.5 * g, g)
        s = spec_ref[part]
        high, low = split(jnp.concatenate([s[:HALF] * g, s[HALF:] * g], 0))
        sums.append(mm(inv_ref[0, part], high) + mm(inv_ref[0, part], low)
                    + mm(inv_ref[1, part], high))
    own = first_channel(per)
    lane = iota((1, 128), 1)
    cosine, sine = twf_ref[0, :HALF].T, twf_ref[1, :HALF].T
    shared_cos, shared_sin = twf_ref[0, HALF:].T[:, 0:1], twf_ref[1, HALF:].T[:, 0:1]
    lane0 = iota((RADIX, HALF), 1) == 0
    outs = []
    for c in range(per):
        cols = slice(HALF * c, HALF * (c + 1))
        top_re, top_im = sums[0][:RADIX, cols], sums[0][RADIX:, cols]
        bot_re, bot_im = sums[1][:RADIX, cols], sums[1][RADIX:, cols]
        re = jnp.where(lane0, top_re, top_re + bot_re)
        im = top_im + bot_im
        out_re = jnp.where(lane0, re, re * cosine - im * sine)
        out_im = jnp.where(lane0, bot_re * shared_cos - bot_im * shared_sin,
                           re * sine + im * cosine)
        high, low = split(jnp.concatenate([out_re, out_im], 1))
        y = (nt(ends_ref[1, :RADIX], high) + nt(ends_ref[1, :RADIX], low)
             + nt(ends_ref[1, RADIX:], high))
        mine = lane == own + c
        skip = jnp.sum(jnp.where(mine, skip_ref[0:1], 0.0), axis=1, keepdims=True)
        gain = jnp.sum(jnp.where(mine, gain_ref[0:1], 0.0), axis=1, keepdims=True)
        spare = jnp.sum(jnp.where(lane == c, nyq_ref[0:1], 0.0), axis=1, keepdims=True)
        x = r_ref[:, block * c : block * (c + 1), :].astype(f32).reshape(RADIX, RADIX)
        y = y + (spare * gain * (1.0 / SEQ)) * twf_ref[2, HALF : HALF + 1] + skip * x
        outs.append(y.reshape(members, block, RADIX))
    out_ref[...] = jnp.concatenate(outs, 1).astype(bf16)


def call(kernel, outs, scratch=(), flops=0, interpret=False):
    vmem = pl.BlockSpec(memory_space=pltpu.VMEM)
    many = isinstance(outs, (list, tuple))

    def run(*args):
        return pl.pallas_call(
            kernel,
            out_shape=outs,
            in_specs=[vmem] * len(args),
            out_specs=[vmem] * len(outs) if many else vmem,
            scratch_shapes=list(scratch),
            compiler_params=pltpu.CompilerParams(vmem_limit_bytes=40 * 1024 * 1024),
        )(*args)

    return run


def exchange(x, axis):
    return lax.all_to_all(x, axis, split_axis=0, concat_axis=0, tiled=True)


def on_device(signal, cond_in, cond_bias, cond_out, skip_gain):
    shape = jax.ShapeDtypeStruct
    ctx, spread, line = ("y", "xh", "core"), ("y", "z", "core"), ("xl", "xh")
    members = lax.axis_size(ctx)
    pieces = lax.axis_size(spread)
    groups = lax.axis_size(line)
    seq_local, chan = signal.shape
    hid = cond_in.shape[1]
    per = chan // members
    block = seq_local // RADIX
    width = HALF * per
    t = tables(tuple(lax.axis_size(name) for name in ("xh", "y", "core")))
    t = {name: jnp.asarray(value) for name, value in t.items()}
    halves = [pltpu.VMEM((chan * block, 128), f32)] * 2
    piece = shape((members, per * block, RADIX), bf16)

    def send(x, axis, dims):
        return exchange(x.astype(f16).reshape(dims), axis).astype(f32).reshape(x.shape)

    packed = call(pack_kernel, piece, halves)(signal)
    received = exchange(packed, ctx)
    feat, spec, nyq, cout, bias, skip = call(
        functools.partial(forward_kernel, per, block),
        [shape((pieces * (TILE + REST), HALF), f32), shape((2, RADIX, width), f32),
         shape((8, 128), f32), shape((hid, chan), bf16),
         shape((8, hid), f32), shape((8, chan), f32)],
        [pltpu.VMEM((width, 2 * RADIX), bf16)] * 4)(
            received, t["ends"], t["twf"], t["second"],
            cond_in.T, cond_out, cond_bias.reshape(1, hid), skip_gain.reshape(1, chan))
    feat = send(feat, spread, (pieces, (TILE + REST) // 2, 2, HALF))
    partial = call(functools.partial(reduce_kernel, per, hid),
                   shape((hid + TILE, STEP * HALF), f32))(feat)
    partial = jnp.broadcast_to(partial[None], (groups,) + partial.shape)
    partial = send(partial, line, partial.shape)
    gain, spare_gain = call(functools.partial(gain_kernel, per, hid),
                            [shape((pieces * TILE, HALF), f32), shape((8, chan), f32)])(
                                partial, feat, bias, cout)
    gain = send(gain, spread, (pieces, TILE, HALF))
    mixed = call(functools.partial(inverse_kernel, per, block), piece)(
        gain, spec, nyq, spare_gain, skip, received, t["inv"], t["twf"], t["ends"])
    mixed = exchange(mixed, ctx)
    return call(unpack_kernel, shape((seq_local, chan), bf16), halves)(mixed)


def solution(mesh):
    fine = Mesh(mesh.devices.reshape(2, -1, 2, 2, mesh.devices.shape[1] // 2),
                ("xh", "y", "core", "xl", "z"))
    ctx, ch = ("xh", "y", "core"), ("xl", "z")
    return jax.shard_map(
        on_device,
        mesh=fine,
        in_specs=(P(ctx, ch), P(ch, None), P(), P(None, ch), P(ch)),
        out_specs=P(ctx, ch),
        check_vma=False,
    )
```

```python
import functools
import math

import jax
import jax.numpy as jnp
import numpy as np
from jax import lax
from jax.experimental import pallas as pl
from jax.experimental.pallas import tpu as pltpu
from jax.sharding import Mesh
from jax.sharding import PartitionSpec as P

f32, bf16, f16 = jnp.float32, jnp.bfloat16, jnp.float16

RADIX = 256
HALF = RADIX // 2
SEQ = RADIX * RADIX
STEP = 2
TILE, REST = 8, 6
GAIN_SCALE = 0.25
IN_SCALE = 2.0**18
OUT_SCALE = 2.0**16


def split_const(values):
    high = values.astype(np.float32).astype(jnp.bfloat16)
    low = (values - high.astype(np.float64)).astype(np.float32).astype(jnp.bfloat16)
    return high, low


@functools.lru_cache(maxsize=None)
def tables(sizes):
    arrival = np.arange(math.prod(sizes)).reshape(sizes).transpose(1, 0, 2).reshape(-1)
    block = RADIX // arrival.size
    position = (arrival[:, None] * block + np.arange(block)).reshape(-1)
    n = np.arange(RADIX, dtype=np.float64)
    k = np.arange(HALF, dtype=np.float64)
    tau = 2.0 * np.pi
    angle = tau * np.outer(k, n) / RADIX
    first = np.concatenate([np.cos(angle), -np.sin(angle)], 0)
    first[HALF] = np.cos(math.pi * n)
    first = np.concatenate(split_const(first[:, position]), 0)
    angle = tau * np.outer(k, n) / SEQ
    cos_f, sin_f = np.cos(angle), np.sin(angle)
    cos_g = cos_f.copy()
    cos_g[0] = 0.0
    shared = tau * n * (HALF + SEQ // 2) / SEQ
    twf = np.stack([cos_f, sin_f, cos_g]).astype(np.float32)
    row0 = np.zeros((3, 8, RADIX))
    row0[0, 0], row0[1, 0] = np.cos(shared), np.sin(shared)
    row0[2, :] = np.cos(math.pi * n)
    twf = np.concatenate([twf, row0.astype(np.float32)], 1)
    angle = tau * np.outer(n, n) / RADIX
    wre, wim = np.cos(angle), -np.sin(angle)
    full = [np.concatenate([wre, -wim], 1), np.concatenate([wim, wre], 1)]
    order = np.arange(HALF).reshape(-1, STEP).T.reshape(-1)
    second = np.stack([np.concatenate([f[order] for f in full], 0),
                       np.concatenate([f[HALF + order] for f in full], 0)])
    second = np.stack(split_const(second))
    vre, vim = np.cos(angle), np.sin(angle)
    inv = np.stack([
        np.concatenate([np.concatenate([vre[:, s], -vim[:, s]], 1),
                        np.concatenate([vim[:, s], vre[:, s]], 1)], 0)
        for s in (order, HALF + order)])
    inv = np.stack(split_const(inv))
    angle = tau * np.outer(n, k) / RADIX
    last = np.concatenate([np.cos(angle), -np.sin(angle)], 1)
    last[:, HALF] = np.cos(math.pi * n)
    last = np.concatenate(split_const(last[position] * (2.0 / SEQ)), 0)
    ends = np.stack([first, last])
    return dict(ends=ends, twf=twf, second=second, inv=inv)


def split(x):
    high = x.astype(bf16)
    return high, (x - high.astype(f32)).astype(bf16)


def mm(a, b):
    return jnp.dot(a, b, preferred_element_type=f32)


def nt(a, b):
    return lax.dot_general(a, b, (((1,), (1,)), ((), ())), preferred_element_type=f32)


def iota(shape, axis):
    return lax.broadcasted_iota(jnp.int32, shape, axis)


def first_channel(per):
    index = lax.axis_index("y") * lax.axis_size("xh") + lax.axis_index("xh")
    return (index * lax.axis_size("core") + lax.axis_index("core")) * per


def pack_kernel(x_ref, out_ref, left, right):
    rows = x_ref.shape[0] // RADIX
    chan = x_ref.shape[1]
    for a in range(rows):
        block = x_ref[RADIX * a : RADIX * (a + 1), :].astype(f32).T
        left[pl.ds(a, chan, stride=rows), :] = block[:, :128]
        right[pl.ds(a, chan, stride=rows), :] = block[:, 128:]
    out_ref[:, :, :128] = left[...].astype(bf16).reshape(out_ref.shape[:2] + (128,))
    out_ref[:, :, 128:] = right[...].astype(bf16).reshape(out_ref.shape[:2] + (128,))


def unpack_kernel(r_ref, out_ref, left, right):
    rows = out_ref.shape[0] // RADIX
    chan = out_ref.shape[1]
    left[...] = r_ref[:, :, :128].astype(f32).reshape(left.shape)
    right[...] = r_ref[:, :, 128:].astype(f32).reshape(right.shape)
    for a in range(rows):
        out_ref[RADIX * a : RADIX * a + 128, :] = (
            left[pl.ds(a, chan, stride=rows), :].T.astype(bf16))
        out_ref[RADIX * a + 128 : RADIX * (a + 1), :] = (
            right[pl.ds(a, chan, stride=rows), :].T.astype(bf16))


def forward_kernel(per, block, r_ref, ends_ref, twf_ref, second_ref,
                   cin_ref, cout_in_ref, bias_in_ref, skip_in_ref,
                   feat_ref, spec_ref, nyq_ref, cout_ref, bias_ref, skip_ref,
                   hi, lo, hi2, lo2):
    cout_ref[...] = cout_in_ref[...]
    bias_ref[...] = jnp.broadcast_to(bias_in_ref[...], bias_ref.shape)
    skip_ref[...] = jnp.broadcast_to(skip_in_ref[...], skip_ref.shape)
    values = r_ref[...].astype(f32)
    first_row = iota((8, RADIX), 0) == 0
    spare = jnp.zeros((8, 128), f32)
    spare_lane = iota((8, 128), 1)
    for c in range(per):
        x = values[:, block * c : block * (c + 1), :].reshape(RADIX, RADIX).astype(bf16)
        a = mm(ends_ref[0], x)
        a = a[:RADIX] + a[RADIX:]
        re, im = a[:HALF], a[HALF:]
        out_re = re * twf_ref[0, :HALF] + im * twf_ref[1, :HALF]
        out_im = im * twf_ref[2, :HALF] - re * twf_ref[1, :HALF]
        place = pl.ds(HALF * c, HALF)
        for at, part in ((0, out_re), (RADIX, out_im)):
            high, low = split(part)
            hi[place, at : at + RADIX], lo[place, at : at + RADIX] = high, low
            hi2[place, at : at + RADIX], lo2[place, at : at + RADIX] = high, low
        lead = im[0:8]
        top = pl.ds(HALF * c, 16)
        alt_re = jnp.concatenate(
            [jnp.where(first_row, lead * twf_ref[0, HALF:], out_re[0:8]), out_re[8:16]], 0)
        alt_im = jnp.concatenate(
            [jnp.where(first_row, -lead * twf_ref[1, HALF:], out_im[0:8]), out_im[8:16]], 0)
        for at, part in ((0, alt_re), (RADIX, alt_im)):
            high, low = split(part)
            hi2[top, at : at + RADIX], lo2[top, at : at + RADIX] = high, low
        nyq = jnp.sum(re[0:1] * twf_ref[2, HALF : HALF + 1], axis=1, keepdims=True)
        spare = jnp.where(spare_lane == c, nyq, spare)
    nyq_ref[...] = spare
    chan = cin_ref.shape[1]
    row = iota((TILE, chan), 0)
    select = ((iota((TILE, chan), 1) == first_channel(per) + row) & (row < per))
    select = select.astype(f32).astype(bf16)
    tile = jnp.concatenate([nt(select, cin_ref[...]) * IN_SCALE,
                            nt(select, cout_in_ref[...]) * OUT_SCALE], 1)
    tile = jnp.where(iota((TILE, 128), 0) == per, jnp.log1p(spare * spare * (1.0 / SEQ)), tile)
    stride = TILE + REST
    pieces = feat_ref.shape[0] // stride
    for r in range(REST):
        feat_ref[pl.ds(TILE + r, pieces, stride=stride), :] = jnp.broadcast_to(
            tile[r : r + 1], (pieces, 128))
    count = HALF // STEP
    for part, (h, l) in enumerate(((hi, lo), (hi2, lo2))):
        s = (nt(second_ref[0, part], h[...]) + nt(second_ref[0, part], l[...])
             + nt(second_ref[1, part], h[...]))
        spec_ref[part] = s
        re, im = s[:HALF], s[HALF:]
        feature = jnp.log1p((re * re + im * im) * (1.0 / SEQ))
        for c in range(per):
            for k in range(STEP):
                feat_ref[pl.ds(part * count * stride + STEP * c + k, count, stride=stride), :] = (
                    feature[count * k : count * (k + 1), HALF * c : HALF * (c + 1)])


def reduce_kernel(per, hid, f_ref, out_ref):
    stride = TILE + REST
    pieces = f_ref.shape[0] // stride

    def rows(r):
        return f_ref[pl.ds(r, pieces, stride=stride), :]

    weights = [rows(TILE + c) for c in range(per)]
    left = jnp.concatenate([w.T[:hid] for w in weights], 1).astype(bf16)
    features = jnp.concatenate(
        [jnp.concatenate([rows(STEP * c + k) for c in range(per)], 0) for k in range(STEP)], 1)
    high, low = split(features)
    pre = mm(left, jnp.concatenate([high, low], 1))
    width = STEP * HALF
    out_ref[:hid] = (pre[:, :width] + pre[:, width:]) * (1.0 / IN_SCALE)
    last = rows(TILE + per)
    extra = weights[0] * last[:, 0:1]
    for c in range(1, per):
        extra = extra + weights[c] * last[:, c : c + 1]
    extra = jnp.sum(extra, axis=0, keepdims=True) * (1.0 / IN_SCALE)
    out_ref[hid:, :128] = jnp.broadcast_to(extra, (TILE, 128))
    out_ref[hid:, 128:] = jnp.zeros((TILE, width - 128), f32)


def gelu(v):
    return 0.5 * v * (1.0 + lax.erf(v * math.sqrt(0.5)))


def gain_kernel(per, hid, r_ref, f_ref, bias_ref, cout_ref, out_ref, gain_ref):
    total = r_ref[0]
    for g in range(1, r_ref.shape[0]):
        total = total + r_ref[g]
    bias = bias_ref[0:1]
    column = jnp.sum(jnp.where(iota((hid, hid), 1) == iota((hid, hid), 0), bias, 0.0),
                     axis=1, keepdims=True)
    high, low = split(gelu(total[:hid] + column))
    hidden = jnp.concatenate([high, low], 1)
    hidden = jnp.concatenate([jnp.zeros_like(hidden), hidden], 0)
    stride = TILE + REST
    pieces = f_ref.shape[0] // stride
    width = STEP * HALF
    for c in range(per):
        weights = f_ref[pl.ds(TILE + c, pieces, stride=stride), :].astype(bf16)
        g = mm(weights, hidden)
        g = (g[:, :width] + g[:, width:]) * (GAIN_SCALE / OUT_SCALE)
        for k in range(STEP):
            out_ref[pl.ds(STEP * c + k, pieces, stride=TILE), :] = g[:, HALF * k : HALF * (k + 1)]
    high, low = split(gelu(total[hid:, :hid] + bias))
    gain_ref[...] = mm(high, cout_ref[...]) + mm(low, cout_ref[...])


def inverse_kernel(per, block, g_ref, spec_ref, nyq_ref, gain_ref, skip_ref, r_ref,
                   inv_ref, twf_ref, ends_ref, out_ref):
    members = r_ref.shape[0]
    width = HALF * per
    count = HALF // STEP
    sums = []
    for part in range(2):
        g = jnp.concatenate([
            jnp.concatenate([
                g_ref[pl.ds(part * count * TILE + STEP * c + k, count, stride=TILE), :]
                for k in range(STEP)], 0)
            for c in range(per)], 1) * (1.0 / GAIN_SCALE)
        if part == 0:
            dc = (iota((HALF, width), 0) == 0) & (iota((HALF, width), 1) % HALF == 0)
            g = jnp.where(dc, 0.5 * g, g)
        s = spec_ref[part]
        high, low = split(jnp.concatenate([s[:HALF] * g, s[HALF:] * g], 0))
        sums.append(mm(inv_ref[0, part], high) + mm(inv_ref[0, part], low)
                    + mm(inv_ref[1, part], high))
    own = first_channel(per)
    lane = iota((1, 128), 1)
    cosine, sine = twf_ref[0, :HALF].T, twf_ref[1, :HALF].T
    shared_cos, shared_sin = twf_ref[0, HALF:].T[:, 0:1], twf_ref[1, HALF:].T[:, 0:1]
    lane0 = iota((RADIX, HALF), 1) == 0
    outs = []
    for c in range(per):
        cols = slice(HALF * c, HALF * (c + 1))
        top_re, top_im = sums[0][:RADIX, cols], sums[0][RADIX:, cols]
        bot_re, bot_im = sums[1][:RADIX, cols], sums[1][RADIX:, cols]
        re = jnp.where(lane0, top_re, top_re + bot_re)
        im = top_im + bot_im
        out_re = jnp.where(lane0, re, re * cosine - im * sine)
        out_im = jnp.where(lane0, bot_re * shared_cos - bot_im * shared_sin,
                           re * sine + im * cosine)
        high, low = split(jnp.concatenate([out_re, out_im], 1))
        y = (nt(ends_ref[1, :RADIX], high) + nt(ends_ref[1, :RADIX], low)
             + nt(ends_ref[1, RADIX:], high))
        mine = lane == own + c
        skip = jnp.sum(jnp.where(mine, skip_ref[0:1], 0.0), axis=1, keepdims=True)
        gain = jnp.sum(jnp.where(mine, gain_ref[0:1], 0.0), axis=1, keepdims=True)
        spare = jnp.sum(jnp.where(lane == c, nyq_ref[0:1], 0.0), axis=1, keepdims=True)
        x = r_ref[:, block * c : block * (c + 1), :].astype(f32).reshape(RADIX, RADIX)
        y = y + (spare * gain * (1.0 / SEQ)) * twf_ref[2, HALF : HALF + 1] + skip * x
        outs.append(y.reshape(members, block, RADIX))
    out_ref[...] = jnp.concatenate(outs, 1).astype(bf16)


def call(kernel, outs, scratch=(), flops=0, interpret=False):
    vmem = pl.BlockSpec(memory_space=pltpu.VMEM)
    many = isinstance(outs, (list, tuple))

    def run(*args):
        return pl.pallas_call(
            kernel,
            out_shape=outs,
            in_specs=[vmem] * len(args),
            out_specs=[vmem] * len(outs) if many else vmem,
            scratch_shapes=list(scratch),
            compiler_params=pltpu.CompilerParams(vmem_limit_bytes=40 * 1024 * 1024),
        )(*args)

    return run


def exchange(x, axis):
    return lax.all_to_all(x, axis, split_axis=0, concat_axis=0, tiled=True)


def on_device(signal, cond_in, cond_bias, cond_out, skip_gain):
    shape = jax.ShapeDtypeStruct
    ctx, spread, line = ("y", "xh", "core"), ("z", "core", "y"), ("xl", "xh")
    members = lax.axis_size(ctx)
    pieces = lax.axis_size(spread)
    groups = lax.axis_size(line)
    seq_local, chan = signal.shape
    hid = cond_in.shape[1]
    per = chan // members
    block = seq_local // RADIX
    width = HALF * per
    t = tables(tuple(lax.axis_size(name) for name in ("xh", "y", "core")))
    t = {name: jnp.asarray(value) for name, value in t.items()}
    halves = [pltpu.VMEM((chan * block, 128), f32)] * 2
    piece = shape((members, per * block, RADIX), bf16)

    def send(x, axis, dims):
        return exchange(x.astype(f16).reshape(dims), axis).astype(f32).reshape(x.shape)

    packed = call(pack_kernel, piece, halves)(signal)
    received = exchange(packed, ctx)
    feat, spec, nyq, cout, bias, skip = call(
        functools.partial(forward_kernel, per, block),
        [shape((pieces * (TILE + REST), HALF), f32), shape((2, RADIX, width), f32),
         shape((8, 128), f32), shape((hid, chan), bf16),
         shape((8, hid), f32), shape((8, chan), f32)],
        [pltpu.VMEM((width, 2 * RADIX), bf16)] * 4)(
            received, t["ends"], t["twf"], t["second"],
            cond_in.T, cond_out, cond_bias.reshape(1, hid), skip_gain.reshape(1, chan))
    feat = send(feat, spread, (pieces, (TILE + REST) // 2, 2, HALF))
    partial = call(functools.partial(reduce_kernel, per, hid),
                   shape((hid + TILE, STEP * HALF), f32))(feat)
    partial = jnp.broadcast_to(partial[None], (groups,) + partial.shape)
    partial = send(partial, line, partial.shape)
    gain, spare_gain = call(functools.partial(gain_kernel, per, hid),
                            [shape((pieces * TILE, HALF), f32), shape((8, chan), f32)])(
                                partial, feat, bias, cout)
    gain = send(gain, spread, (pieces, TILE, HALF))
    mixed = call(functools.partial(inverse_kernel, per, block), piece)(
        gain, spec, nyq, spare_gain, skip, received, t["inv"], t["twf"], t["ends"])
    mixed = exchange(mixed, ctx)
    return call(unpack_kernel, shape((seq_local, chan), bf16), halves)(mixed)


def solution(mesh):
    fine = Mesh(mesh.devices.reshape(2, -1, 2, 2, mesh.devices.shape[1] // 2),
                ("xh", "y", "core", "xl", "z"))
    ctx, ch = ("xh", "y", "core"), ("xl", "z")
    return jax.shard_map(
        on_device,
        mesh=fine,
        in_specs=(P(ctx, ch), P(ch, None), P(), P(None, ch), P(ch)),
        out_specs=P(ctx, ch),
        check_vma=False,
    )
```

```python
import functools
import math

import jax
import jax.numpy as jnp
import numpy as np
from jax import lax
from jax.experimental import pallas as pl
from jax.experimental.pallas import tpu as pltpu
from jax.sharding import Mesh
from jax.sharding import PartitionSpec as P

f32, bf16, f16 = jnp.float32, jnp.bfloat16, jnp.float16

RADIX = 256
HALF = RADIX // 2
SEQ = RADIX * RADIX
STEP = 2
TILE, REST = 8, 6
GAIN_SCALE = 0.25
IN_SCALE = 2.0**18
OUT_SCALE = 2.0**16


def split_const(values):
    high = values.astype(np.float32).astype(jnp.bfloat16)
    low = (values - high.astype(np.float64)).astype(np.float32).astype(jnp.bfloat16)
    return high, low


@functools.lru_cache(maxsize=None)
def tables(sizes):
    arrival = np.arange(math.prod(sizes)).reshape(sizes).transpose(1, 0, 2).reshape(-1)
    block = RADIX // arrival.size
    position = (arrival[:, None] * block + np.arange(block)).reshape(-1)
    n = np.arange(RADIX, dtype=np.float64)
    k = np.arange(HALF, dtype=np.float64)
    tau = 2.0 * np.pi
    angle = tau * np.outer(k, n) / RADIX
    first = np.concatenate([np.cos(angle), -np.sin(angle)], 0)
    first[HALF] = np.cos(math.pi * n)
    first = np.concatenate(split_const(first[:, position]), 0)
    angle = tau * np.outer(k, n) / SEQ
    cos_f, sin_f = np.cos(angle), np.sin(angle)
    cos_g = cos_f.copy()
    cos_g[0] = 0.0
    shared = tau * n * (HALF + SEQ // 2) / SEQ
    twf = np.stack([cos_f, sin_f, cos_g]).astype(np.float32)
    row0 = np.zeros((3, 8, RADIX))
    row0[0, 0], row0[1, 0] = np.cos(shared), np.sin(shared)
    row0[2, :] = np.cos(math.pi * n)
    twf = np.concatenate([twf, row0.astype(np.float32)], 1)
    angle = tau * np.outer(n, n) / RADIX
    wre, wim = np.cos(angle), -np.sin(angle)
    full = [np.concatenate([wre, -wim], 1), np.concatenate([wim, wre], 1)]
    order = np.arange(HALF).reshape(-1, STEP).T.reshape(-1)
    second = np.stack([np.concatenate([f[order] for f in full], 0),
                       np.concatenate([f[HALF + order] for f in full], 0)])
    second = np.stack(split_const(second))
    vre, vim = np.cos(angle), np.sin(angle)
    inv = np.stack([
        np.concatenate([np.concatenate([vre[:, s], -vim[:, s]], 1),
                        np.concatenate([vim[:, s], vre[:, s]], 1)], 0)
        for s in (order, HALF + order)])
    inv = np.stack(split_const(inv))
    angle = tau * np.outer(n, k) / RADIX
    last = np.concatenate([np.cos(angle), -np.sin(angle)], 1)
    last[:, HALF] = np.cos(math.pi * n)
    last = np.concatenate(split_const(last[position] * (2.0 / SEQ)), 0)
    ends = np.stack([first, last])
    return dict(ends=ends, twf=twf, second=second, inv=inv)


def split(x):
    high = x.astype(bf16)
    return high, (x - high.astype(f32)).astype(bf16)


def mm(a, b):
    return jnp.dot(a, b, preferred_element_type=f32)


def nt(a, b):
    return lax.dot_general(a, b, (((1,), (1,)), ((), ())), preferred_element_type=f32)


def iota(shape, axis):
    return lax.broadcasted_iota(jnp.int32, shape, axis)


def first_channel(per):
    index = lax.axis_index("y") * lax.axis_size("xh") + lax.axis_index("xh")
    return (index * lax.axis_size("core") + lax.axis_index("core")) * per


def pack_kernel(x_ref, out_ref, left, right):
    rows = x_ref.shape[0] // RADIX
    chan = x_ref.shape[1]
    for a in range(rows):
        block = x_ref[RADIX * a : RADIX * (a + 1), :].astype(f32).T
        left[pl.ds(a, chan, stride=rows), :] = block[:, :128]
        right[pl.ds(a, chan, stride=rows), :] = block[:, 128:]
    out_ref[:, :, :128] = left[...].astype(bf16).reshape(out_ref.shape[:2] + (128,))
    out_ref[:, :, 128:] = right[...].astype(bf16).reshape(out_ref.shape[:2] + (128,))


def unpack_kernel(r_ref, out_ref, left, right):
    rows = out_ref.shape[0] // RADIX
    chan = out_ref.shape[1]
    left[...] = r_ref[:, :, :128].astype(f32).reshape(left.shape)
    right[...] = r_ref[:, :, 128:].astype(f32).reshape(right.shape)
    for a in range(rows):
        out_ref[RADIX * a : RADIX * a + 128, :] = (
            left[pl.ds(a, chan, stride=rows), :].T.astype(bf16))
        out_ref[RADIX * a + 128 : RADIX * (a + 1), :] = (
            right[pl.ds(a, chan, stride=rows), :].T.astype(bf16))


def forward_kernel(per, block, r_ref, ends_ref, twf_ref, second_ref,
                   cin_ref, cout_in_ref, bias_in_ref, skip_in_ref,
                   feat_ref, spec_ref, nyq_ref, cout_ref, bias_ref, skip_ref,
                   hi, lo, hi2, lo2):
    cout_ref[...] = cout_in_ref[...]
    bias_ref[...] = jnp.broadcast_to(bias_in_ref[...], bias_ref.shape)
    skip_ref[...] = jnp.broadcast_to(skip_in_ref[...], skip_ref.shape)
    values = r_ref[...].astype(f32)
    first_row = iota((8, RADIX), 0) == 0
    spare = jnp.zeros((8, 128), f32)
    spare_lane = iota((8, 128), 1)
    for c in range(per):
        x = values[:, block * c : block * (c + 1), :].reshape(RADIX, RADIX).astype(bf16)
        a = mm(ends_ref[0], x)
        a = a[:RADIX] + a[RADIX:]
        re, im = a[:HALF], a[HALF:]
        out_re = re * twf_ref[0, :HALF] + im * twf_ref[1, :HALF]
        out_im = im * twf_ref[2, :HALF] - re * twf_ref[1, :HALF]
        place = pl.ds(HALF * c, HALF)
        for at, part in ((0, out_re), (RADIX, out_im)):
            high, low = split(part)
            hi[place, at : at + RADIX], lo[place, at : at + RADIX] = high, low
        lead = im[0:8]
        top = pl.ds(16 * c, 16)
        alt_re = jnp.concatenate(
            [jnp.where(first_row, lead * twf_ref[0, HALF:], out_re[0:8]), out_re[8:16]], 0)
        alt_im = jnp.concatenate(
            [jnp.where(first_row, -lead * twf_ref[1, HALF:], out_im[0:8]), out_im[8:16]], 0)
        for at, part in ((0, alt_re), (RADIX, alt_im)):
            high, low = split(part)
            hi2[top, at : at + RADIX], lo2[top, at : at + RADIX] = high, low
        nyq = jnp.sum(re[0:1] * twf_ref[2, HALF : HALF + 1], axis=1, keepdims=True)
        spare = jnp.where(spare_lane == c, nyq, spare)
    nyq_ref[...] = spare
    chan = cin_ref.shape[1]
    row = iota((TILE, chan), 0)
    select = ((iota((TILE, chan), 1) == first_channel(per) + row) & (row < per))
    select = select.astype(f32).astype(bf16)
    tile = jnp.concatenate([nt(select, cin_ref[...]) * IN_SCALE,
                            nt(select, cout_in_ref[...]) * OUT_SCALE], 1)
    tile = jnp.where(iota((TILE, 128), 0) == per, jnp.log1p(spare * spare * (1.0 / SEQ)), tile)
    stride = TILE + REST
    pieces = feat_ref.shape[0] // stride
    for r in range(REST):
        feat_ref[pl.ds(TILE + r, pieces, stride=stride), :] = jnp.broadcast_to(
            tile[r : r + 1], (pieces, 128))
    count = HALF // STEP
    for part in range(2):
        if part:
            for c in range(per):
                top, place = pl.ds(16 * c, 16), pl.ds(HALF * c, 16)
                hi[place], lo[place] = hi2[top], lo2[top]
        s = (nt(second_ref[0, part], hi[...]) + nt(second_ref[0, part], lo[...])
             + nt(second_ref[1, part], hi[...]))
        spec_ref[part] = s
        re, im = s[:HALF], s[HALF:]
        feature = jnp.log1p((re * re + im * im) * (1.0 / SEQ))
        for c in range(per):
            for k in range(STEP):
                feat_ref[pl.ds(part * count * stride + STEP * c + k, count, stride=stride), :] = (
                    feature[count * k : count * (k + 1), HALF * c : HALF * (c + 1)])


def reduce_kernel(per, hid, f_ref, out_ref):
    stride = TILE + REST
    pieces = f_ref.shape[0] // stride

    def rows(r):
        return f_ref[pl.ds(r, pieces, stride=stride), :]

    weights = [rows(TILE + c) for c in range(per)]
    left = jnp.concatenate([w.T[:hid] for w in weights], 1).astype(bf16)
    features = jnp.concatenate(
        [jnp.concatenate([rows(STEP * c + k) for c in range(per)], 0) for k in range(STEP)], 1)
    high, low = split(features)
    pre = mm(left, jnp.concatenate([high, low], 1))
    width = STEP * HALF
    out_ref[:hid] = (pre[:, :width] + pre[:, width:]) * (1.0 / IN_SCALE)
    last = rows(TILE + per)
    extra = weights[0] * last[:, 0:1]
    for c in range(1, per):
        extra = extra + weights[c] * last[:, c : c + 1]
    extra = jnp.sum(extra, axis=0, keepdims=True) * (1.0 / IN_SCALE)
    out_ref[hid:, :128] = jnp.broadcast_to(extra, (TILE, 128))
    out_ref[hid:, 128:] = jnp.zeros((TILE, width - 128), f32)


def gelu(v):
    return 0.5 * v * (1.0 + lax.erf(v * math.sqrt(0.5)))


def gain_kernel(per, hid, r_ref, f_ref, bias_ref, cout_ref, out_ref, gain_ref):
    total = r_ref[0]
    for g in range(1, r_ref.shape[0]):
        total = total + r_ref[g]
    bias = bias_ref[0:1]
    column = jnp.sum(jnp.where(iota((hid, hid), 1) == iota((hid, hid), 0), bias, 0.0),
                     axis=1, keepdims=True)
    high, low = split(gelu(total[:hid] + column))
    hidden = jnp.concatenate([high, low], 1)
    hidden = jnp.concatenate([jnp.zeros_like(hidden), hidden], 0)
    stride = TILE + REST
    pieces = f_ref.shape[0] // stride
    width = STEP * HALF
    for c in range(per):
        weights = f_ref[pl.ds(TILE + c, pieces, stride=stride), :].astype(bf16)
        g = mm(weights, hidden)
        g = (g[:, :width] + g[:, width:]) * (GAIN_SCALE / OUT_SCALE)
        for k in range(STEP):
            out_ref[pl.ds(STEP * c + k, pieces, stride=TILE), :] = g[:, HALF * k : HALF * (k + 1)]
    high, low = split(gelu(total[hid:, :hid] + bias))
    gain_ref[...] = mm(high, cout_ref[...]) + mm(low, cout_ref[...])


def inverse_kernel(per, block, g_ref, spec_ref, nyq_ref, gain_ref, skip_ref, r_ref,
                   inv_ref, twf_ref, ends_ref, out_ref):
    members = r_ref.shape[0]
    width = HALF * per
    count = HALF // STEP
    sums = []
    for part in range(2):
        g = jnp.concatenate([
            jnp.concatenate([
                g_ref[pl.ds(part * count * TILE + STEP * c + k, count, stride=TILE), :]
                for k in range(STEP)], 0)
            for c in range(per)], 1) * (1.0 / GAIN_SCALE)
        if part == 0:
            dc = (iota((HALF, width), 0) == 0) & (iota((HALF, width), 1) % HALF == 0)
            g = jnp.where(dc, 0.5 * g, g)
        s = spec_ref[part]
        high, low = split(jnp.concatenate([s[:HALF] * g, s[HALF:] * g], 0))
        sums.append(mm(inv_ref[0, part], high) + mm(inv_ref[0, part], low)
                    + mm(inv_ref[1, part], high))
    own = first_channel(per)
    lane = iota((1, 128), 1)
    cosine, sine = twf_ref[0, :HALF].T, twf_ref[1, :HALF].T
    shared_cos, shared_sin = twf_ref[0, HALF:].T[:, 0:1], twf_ref[1, HALF:].T[:, 0:1]
    lane0 = iota((RADIX, HALF), 1) == 0
    outs = []
    for c in range(per):
        cols = slice(HALF * c, HALF * (c + 1))
        top_re, top_im = sums[0][:RADIX, cols], sums[0][RADIX:, cols]
        bot_re, bot_im = sums[1][:RADIX, cols], sums[1][RADIX:, cols]
        re = jnp.where(lane0, top_re, top_re + bot_re)
        im = top_im + bot_im
        out_re = jnp.where(lane0, re, re * cosine - im * sine)
        out_im = jnp.where(lane0, bot_re * shared_cos - bot_im * shared_sin,
                           re * sine + im * cosine)
        high, low = split(jnp.concatenate([out_re, out_im], 1))
        y = (nt(ends_ref[1, :RADIX], high) + nt(ends_ref[1, :RADIX], low)
             + nt(ends_ref[1, RADIX:], high))
        mine = lane == own + c
        skip = jnp.sum(jnp.where(mine, skip_ref[0:1], 0.0), axis=1, keepdims=True)
        gain = jnp.sum(jnp.where(mine, gain_ref[0:1], 0.0), axis=1, keepdims=True)
        spare = jnp.sum(jnp.where(lane == c, nyq_ref[0:1], 0.0), axis=1, keepdims=True)
        x = r_ref[:, block * c : block * (c + 1), :].astype(f32).reshape(RADIX, RADIX)
        y = y + (spare * gain * (1.0 / SEQ)) * twf_ref[2, HALF : HALF + 1] + skip * x
        outs.append(y.reshape(members, block, RADIX))
    out_ref[...] = jnp.concatenate(outs, 1).astype(bf16)


def call(kernel, outs, scratch=(), flops=0, interpret=False):
    vmem = pl.BlockSpec(memory_space=pltpu.VMEM)
    many = isinstance(outs, (list, tuple))

    def run(*args):
        return pl.pallas_call(
            kernel,
            out_shape=outs,
            in_specs=[vmem] * len(args),
            out_specs=[vmem] * len(outs) if many else vmem,
            scratch_shapes=list(scratch),
            compiler_params=pltpu.CompilerParams(vmem_limit_bytes=40 * 1024 * 1024),
        )(*args)

    return run


def exchange(x, axis):
    return lax.all_to_all(x, axis, split_axis=0, concat_axis=0, tiled=True)


def on_device(signal, cond_in, cond_bias, cond_out, skip_gain):
    shape = jax.ShapeDtypeStruct
    ctx, spread, line = ("y", "xh", "core"), ("z", "core", "y"), ("xl", "xh")
    members = lax.axis_size(ctx)
    pieces = lax.axis_size(spread)
    groups = lax.axis_size(line)
    seq_local, chan = signal.shape
    hid = cond_in.shape[1]
    per = chan // members
    block = seq_local // RADIX
    width = HALF * per
    t = tables(tuple(lax.axis_size(name) for name in ("xh", "y", "core")))
    t = {name: jnp.asarray(value) for name, value in t.items()}
    halves = [pltpu.VMEM((chan * block, 128), f32)] * 2
    piece = shape((members, per * block, RADIX), bf16)

    def send(x, axis, dims):
        return exchange(x.astype(f16).reshape(dims), axis).astype(f32).reshape(x.shape)

    packed = call(pack_kernel, piece, halves)(signal)
    received = exchange(packed, ctx)
    feat, spec, nyq, cout, bias, skip = call(
        functools.partial(forward_kernel, per, block),
        [shape((pieces * (TILE + REST), HALF), f32), shape((2, RADIX, width), f32),
         shape((8, 128), f32), shape((hid, chan), bf16),
         shape((8, hid), f32), shape((8, chan), f32)],
        [pltpu.VMEM((width, 2 * RADIX), bf16)] * 2
        + [pltpu.VMEM((16 * per, 2 * RADIX), bf16)] * 2)(
            received, t["ends"], t["twf"], t["second"],
            cond_in.T, cond_out, cond_bias.reshape(1, hid), skip_gain.reshape(1, chan))
    feat = send(feat, spread, (pieces, (TILE + REST) // 2, 2, HALF))
    partial = call(functools.partial(reduce_kernel, per, hid),
                   shape((hid + TILE, STEP * HALF), f32))(feat)
    partial = jnp.broadcast_to(partial[None], (groups,) + partial.shape)
    partial = send(partial, line, partial.shape)
    gain, spare_gain = call(functools.partial(gain_kernel, per, hid),
                            [shape((pieces * TILE, HALF), f32), shape((8, chan), f32)])(
                                partial, feat, bias, cout)
    gain = send(gain, spread, (pieces, TILE, HALF))
    mixed = call(functools.partial(inverse_kernel, per, block), piece)(
        gain, spec, nyq, spare_gain, skip, received, t["inv"], t["twf"], t["ends"])
    mixed = exchange(mixed, ctx)
    return call(unpack_kernel, shape((seq_local, chan), bf16), halves)(mixed)


def solution(mesh):
    fine = Mesh(mesh.devices.reshape(2, -1, 2, 2, mesh.devices.shape[1] // 2),
                ("xh", "y", "core", "xl", "z"))
    ctx, ch = ("xh", "y", "core"), ("xl", "z")
    return jax.shard_map(
        on_device,
        mesh=fine,
        in_specs=(P(ctx, ch), P(ch, None), P(), P(None, ch), P(ch)),
        out_specs=P(ctx, ch),
        check_vma=False,
    )
```

```python
import functools
import math

import jax
import jax.numpy as jnp
import numpy as np
from jax import lax
from jax.experimental import pallas as pl
from jax.experimental.pallas import tpu as pltpu
from jax.sharding import Mesh
from jax.sharding import PartitionSpec as P

f32, bf16, f16 = jnp.float32, jnp.bfloat16, jnp.float16

RADIX = 256
HALF = RADIX // 2
SEQ = RADIX * RADIX
STEP = 2
TILE, REST = 8, 6
GAIN_SCALE = 0.25
IN_SCALE = 2.0**18
OUT_SCALE = 2.0**16


def split_const(values):
    high = values.astype(np.float32).astype(jnp.bfloat16)
    low = (values - high.astype(np.float64)).astype(np.float32).astype(jnp.bfloat16)
    return high, low


@functools.lru_cache(maxsize=None)
def tables(sizes):
    arrival = np.arange(math.prod(sizes)).reshape(sizes).transpose(1, 0, 2).reshape(-1)
    block = RADIX // arrival.size
    position = (arrival[:, None] * block + np.arange(block)).reshape(-1)
    n = np.arange(RADIX, dtype=np.float64)
    k = np.arange(HALF, dtype=np.float64)
    tau = 2.0 * np.pi
    angle = tau * np.outer(k, n) / RADIX
    first = np.concatenate([np.cos(angle), -np.sin(angle)], 0)
    first[HALF] = np.cos(math.pi * n)
    first = np.concatenate(split_const(first[:, position]), 0)
    angle = tau * np.outer(k, n) / SEQ
    cos_f, sin_f = np.cos(angle), np.sin(angle)
    cos_g = cos_f.copy()
    cos_g[0] = 0.0
    shared = tau * n * (HALF + SEQ // 2) / SEQ
    twf = np.stack([cos_f, sin_f, cos_g]).astype(np.float32)
    row0 = np.zeros((3, 8, RADIX))
    row0[0, 0], row0[1, 0] = np.cos(shared), np.sin(shared)
    row0[2, :] = np.cos(math.pi * n)
    twf = np.concatenate([twf, row0.astype(np.float32)], 1)
    angle = tau * np.outer(n, n) / RADIX
    wre, wim = np.cos(angle), -np.sin(angle)
    full = [np.concatenate([wre, -wim], 1), np.concatenate([wim, wre], 1)]
    order = np.arange(HALF).reshape(-1, STEP).T.reshape(-1)
    second = np.stack([np.concatenate([f[order] for f in full], 0),
                       np.concatenate([f[HALF + order] for f in full], 0)])
    second = np.stack(split_const(second))
    vre, vim = np.cos(angle), np.sin(angle)
    inv = np.stack([
        np.concatenate([np.concatenate([vre[:, s], -vim[:, s]], 1),
                        np.concatenate([vim[:, s], vre[:, s]], 1)], 0)
        for s in (order, HALF + order)])
    inv = np.stack(split_const(inv))
    angle = tau * np.outer(n, k) / RADIX
    last = np.concatenate([np.cos(angle), -np.sin(angle)], 1)
    last[:, HALF] = np.cos(math.pi * n)
    last = np.concatenate(split_const(last[position] * (2.0 / SEQ)), 0)
    ends = np.stack([first, last])
    return dict(ends=ends, twf=twf, second=second, inv=inv)


def split(x):
    high = x.astype(bf16)
    return high, (x - high.astype(f32)).astype(bf16)


def mm(a, b):
    return jnp.dot(a, b, preferred_element_type=f32)


def nt(a, b):
    return lax.dot_general(a, b, (((1,), (1,)), ((), ())), preferred_element_type=f32)


def iota(shape, axis):
    return lax.broadcasted_iota(jnp.int32, shape, axis)


def first_channel(per):
    index = lax.axis_index("y") * lax.axis_size("xh") + lax.axis_index("xh")
    return (index * lax.axis_size("core") + lax.axis_index("core")) * per


def pack_kernel(x_ref, out_ref, left, right):
    rows = x_ref.shape[0] // RADIX
    chan = x_ref.shape[1]
    for a in range(rows):
        block = x_ref[RADIX * a : RADIX * (a + 1), :].astype(f32).T
        left[pl.ds(a, chan, stride=rows), :] = block[:, :128]
        right[pl.ds(a, chan, stride=rows), :] = block[:, 128:]
    out_ref[:, :, :128] = left[...].astype(bf16).reshape(out_ref.shape[:2] + (128,))
    out_ref[:, :, 128:] = right[...].astype(bf16).reshape(out_ref.shape[:2] + (128,))


def unpack_kernel(r_ref, out_ref, left, right):
    rows = out_ref.shape[0] // RADIX
    chan = out_ref.shape[1]
    left[...] = r_ref[:, :, :128].astype(f32).reshape(left.shape)
    right[...] = r_ref[:, :, 128:].astype(f32).reshape(right.shape)
    for a in range(rows):
        out_ref[RADIX * a : RADIX * a + 128, :] = (
            left[pl.ds(a, chan, stride=rows), :].T.astype(bf16))
        out_ref[RADIX * a + 128 : RADIX * (a + 1), :] = (
            right[pl.ds(a, chan, stride=rows), :].T.astype(bf16))


def forward_kernel(per, block, r_ref, ends_ref, twf_ref, second_ref,
                   cin_ref, cout_in_ref, bias_in_ref, skip_in_ref,
                   feat_ref, spec_ref, nyq_ref, cout_ref, bias_ref, skip_ref,
                   hi, lo, hi2, lo2):
    cout_ref[...] = cout_in_ref[...]
    bias_ref[...] = jnp.broadcast_to(bias_in_ref[...], bias_ref.shape)
    skip_ref[...] = jnp.broadcast_to(skip_in_ref[...], skip_ref.shape)
    values = r_ref[...].astype(f32)
    first_row = iota((8, RADIX), 0) == 0
    spare = jnp.zeros((8, 128), f32)
    spare_lane = iota((8, 128), 1)
    for c in range(per):
        x = values[:, block * c : block * (c + 1), :].reshape(RADIX, RADIX).astype(bf16)
        a = mm(ends_ref[0], x)
        a = a[:RADIX] + a[RADIX:]
        re, im = a[:HALF], a[HALF:]
        out_re = re * twf_ref[0, :HALF] + im * twf_ref[1, :HALF]
        out_im = im * twf_ref[2, :HALF] - re * twf_ref[1, :HALF]
        place = pl.ds(HALF * c, HALF)
        for at, part in ((0, out_re), (RADIX, out_im)):
            high, low = split(part)
            hi[place, at : at + RADIX], lo[place, at : at + RADIX] = high, low
            hi2[place, at : at + RADIX], lo2[place, at : at + RADIX] = high, low
        lead = im[0:8]
        top = pl.ds(HALF * c, 16)
        alt_re = jnp.concatenate(
            [jnp.where(first_row, lead * twf_ref[0, HALF:], out_re[0:8]), out_re[8:16]], 0)
        alt_im = jnp.concatenate(
            [jnp.where(first_row, -lead * twf_ref[1, HALF:], out_im[0:8]), out_im[8:16]], 0)
        for at, part in ((0, alt_re), (RADIX, alt_im)):
            high, low = split(part)
            hi2[top, at : at + RADIX], lo2[top, at : at + RADIX] = high, low
        nyq = jnp.sum(re[0:1] * twf_ref[2, HALF : HALF + 1], axis=1, keepdims=True)
        spare = jnp.where(spare_lane == c, nyq, spare)
    nyq_ref[...] = spare
    chan = cin_ref.shape[1]
    row = iota((TILE, chan), 0)
    select = ((iota((TILE, chan), 1) == first_channel(per) + row) & (row < per))
    select = select.astype(f32).astype(bf16)
    tile = jnp.concatenate([nt(select, cin_ref[...]) * IN_SCALE,
                            nt(select, cout_in_ref[...]) * OUT_SCALE], 1)
    tile = jnp.where(iota((TILE, 128), 0) == per, jnp.log1p(spare * spare * (1.0 / SEQ)), tile)
    stride = TILE + REST
    pieces = feat_ref.shape[0] // stride
    for r in range(REST):
        feat_ref[pl.ds(TILE + r, pieces, stride=stride), :] = jnp.broadcast_to(
            tile[r : r + 1], (pieces, 128))
    count = HALF // STEP
    for part, (h, l) in enumerate(((hi, lo), (hi2, lo2))):
        s = (nt(second_ref[0, part], h[...]) + nt(second_ref[0, part], l[...])
             + nt(second_ref[1, part], h[...]))
        spec_ref[part] = s
        re, im = s[:HALF], s[HALF:]
        feature = jnp.log1p((re * re + im * im) * (1.0 / SEQ))
        for c in range(per):
            for k in range(STEP):
                feat_ref[pl.ds(part * count * stride + STEP * c + k, count, stride=stride), :] = (
                    feature[count * k : count * (k + 1), HALF * c : HALF * (c + 1)])


def reduce_kernel(per, hid, f_ref, out_ref):
    stride = TILE + REST
    pieces = f_ref.shape[0] // stride

    def rows(r):
        return f_ref[pl.ds(r, pieces, stride=stride), :]

    weights = [rows(TILE + c) for c in range(per)]
    left = jnp.concatenate([w.T[:hid] for w in weights], 1).astype(bf16)
    features = jnp.concatenate(
        [jnp.concatenate([rows(STEP * c + k) for c in range(per)], 0) for k in range(STEP)], 1)
    high, low = split(features)
    pre = mm(left, jnp.concatenate([high, low], 1))
    width = STEP * HALF
    out_ref[:hid] = (pre[:, :width] + pre[:, width:]) * (1.0 / IN_SCALE)
    last = rows(TILE + per)
    extra = weights[0] * last[:, 0:1]
    for c in range(1, per):
        extra = extra + weights[c] * last[:, c : c + 1]
    extra = jnp.sum(extra, axis=0, keepdims=True) * (1.0 / IN_SCALE)
    out_ref[hid:, :128] = jnp.broadcast_to(extra, (STEP, 128))
    out_ref[hid:, 128:] = jnp.zeros((STEP, width - 128), f32)


def gelu(v):
    return 0.5 * v * (1.0 + lax.erf(v * math.sqrt(0.5)))


def gain_kernel(per, hid, r_ref, f_ref, bias_ref, cout_ref, out_ref, gain_ref):
    total = r_ref[0]
    for g in range(1, r_ref.shape[0]):
        total = total + r_ref[g]
    bias = bias_ref[0:1]
    column = jnp.sum(jnp.where(iota((hid, hid), 1) == iota((hid, hid), 0), bias, 0.0),
                     axis=1, keepdims=True)
    high, low = split(gelu(total[:hid] + column))
    hidden = jnp.concatenate([high, low], 1)
    hidden = jnp.concatenate([jnp.zeros_like(hidden), hidden], 0)
    stride = TILE + REST
    pieces = f_ref.shape[0] // stride
    width = STEP * HALF
    for c in range(per):
        weights = f_ref[pl.ds(TILE + c, pieces, stride=stride), :].astype(bf16)
        g = mm(weights, hidden)
        g = (g[:, :width] + g[:, width:]) * (GAIN_SCALE / OUT_SCALE)
        for k in range(STEP):
            out_ref[pl.ds(STEP * c + k, pieces, stride=TILE), :] = g[:, HALF * k : HALF * (k + 1)]
    high, low = split(gelu(total[hid:, :hid] + bias))
    gain_ref[...] = mm(high, cout_ref[...]) + mm(low, cout_ref[...])


def inverse_kernel(per, block, g_ref, spec_ref, nyq_ref, gain_ref, skip_ref, r_ref,
                   inv_ref, twf_ref, ends_ref, out_ref):
    members = r_ref.shape[0]
    width = HALF * per
    count = HALF // STEP
    sums = []
    for part in range(2):
        g = jnp.concatenate([
            jnp.concatenate([
                g_ref[pl.ds(part * count * TILE + STEP * c + k, count, stride=TILE), :]
                for k in range(STEP)], 0)
            for c in range(per)], 1) * (1.0 / GAIN_SCALE)
        if part == 0:
            dc = (iota((HALF, width), 0) == 0) & (iota((HALF, width), 1) % HALF == 0)
            g = jnp.where(dc, 0.5 * g, g)
        s = spec_ref[part]
        high, low = split(jnp.concatenate([s[:HALF] * g, s[HALF:] * g], 0))
        sums.append(mm(inv_ref[0, part], high) + mm(inv_ref[0, part], low)
                    + mm(inv_ref[1, part], high))
    own = first_channel(per)
    lane = iota((1, 128), 1)
    cosine, sine = twf_ref[0, :HALF].T, twf_ref[1, :HALF].T
    shared_cos, shared_sin = twf_ref[0, HALF:].T[:, 0:1], twf_ref[1, HALF:].T[:, 0:1]
    lane0 = iota((RADIX, HALF), 1) == 0
    outs = []
    for c in range(per):
        cols = slice(HALF * c, HALF * (c + 1))
        top_re, top_im = sums[0][:RADIX, cols], sums[0][RADIX:, cols]
        bot_re, bot_im = sums[1][:RADIX, cols], sums[1][RADIX:, cols]
        re = jnp.where(lane0, top_re, top_re + bot_re)
        im = top_im + bot_im
        out_re = jnp.where(lane0, re, re * cosine - im * sine)
        out_im = jnp.where(lane0, bot_re * shared_cos - bot_im * shared_sin,
                           re * sine + im * cosine)
        high, low = split(jnp.concatenate([out_re, out_im], 1))
        y = (nt(ends_ref[1, :RADIX], high) + nt(ends_ref[1, :RADIX], low)
             + nt(ends_ref[1, RADIX:], high))
        mine = lane == own + c
        skip = jnp.sum(jnp.where(mine, skip_ref[0:1], 0.0), axis=1, keepdims=True)
        gain = jnp.sum(jnp.where(mine, gain_ref[0:1], 0.0), axis=1, keepdims=True)
        spare = jnp.sum(jnp.where(lane == c, nyq_ref[0:1], 0.0), axis=1, keepdims=True)
        x = r_ref[:, block * c : block * (c + 1), :].astype(f32).reshape(RADIX, RADIX)
        y = y + (spare * gain * (1.0 / SEQ)) * twf_ref[2, HALF : HALF + 1] + skip * x
        outs.append(y.reshape(members, block, RADIX))
    out_ref[...] = jnp.concatenate(outs, 1).astype(bf16)


def call(kernel, outs, scratch=(), flops=0, interpret=False):
    vmem = pl.BlockSpec(memory_space=pltpu.VMEM)
    many = isinstance(outs, (list, tuple))

    def run(*args):
        return pl.pallas_call(
            kernel,
            out_shape=outs,
            in_specs=[vmem] * len(args),
            out_specs=[vmem] * len(outs) if many else vmem,
            scratch_shapes=list(scratch),
            compiler_params=pltpu.CompilerParams(vmem_limit_bytes=40 * 1024 * 1024),
        )(*args)

    return run


def exchange(x, axis):
    return lax.all_to_all(x, axis, split_axis=0, concat_axis=0, tiled=True)


def on_device(signal, cond_in, cond_bias, cond_out, skip_gain):
    shape = jax.ShapeDtypeStruct
    ctx, spread, line = ("y", "xh", "core"), ("z", "core", "y"), ("xl", "xh")
    members = lax.axis_size(ctx)
    pieces = lax.axis_size(spread)
    groups = lax.axis_size(line)
    seq_local, chan = signal.shape
    hid = cond_in.shape[1]
    per = chan // members
    block = seq_local // RADIX
    width = HALF * per
    t = tables(tuple(lax.axis_size(name) for name in ("xh", "y", "core")))
    t = {name: jnp.asarray(value) for name, value in t.items()}
    halves = [pltpu.VMEM((chan * block, 128), f32)] * 2
    piece = shape((members, per * block, RADIX), bf16)

    def send(x, axis, dims):
        return exchange(x.astype(f16).reshape(dims), axis).astype(f32).reshape(x.shape)

    packed = call(pack_kernel, piece, halves)(signal)
    received = exchange(packed, ctx)
    feat, spec, nyq, cout, bias, skip = call(
        functools.partial(forward_kernel, per, block),
        [shape((pieces * (TILE + REST), HALF), f32), shape((2, RADIX, width), f32),
         shape((8, 128), f32), shape((hid, chan), bf16),
         shape((8, hid), f32), shape((8, chan), f32)],
        [pltpu.VMEM((width, 2 * RADIX), bf16)] * 4)(
            received, t["ends"], t["twf"], t["second"],
            cond_in.T, cond_out, cond_bias.reshape(1, hid), skip_gain.reshape(1, chan))
    feat = send(feat, spread, (pieces, (TILE + REST) // 2, 2, HALF))
    partial = call(functools.partial(reduce_kernel, per, hid),
                   shape((hid + STEP, STEP * HALF), f32))(feat)
    partial = jnp.broadcast_to(partial[None], (groups,) + partial.shape)
    partial = send(partial, line, (groups, -1, STEP, STEP * HALF))
    gain, spare_gain = call(functools.partial(gain_kernel, per, hid),
                            [shape((pieces * TILE, HALF), f32), shape((STEP, chan), f32)])(
                                partial, feat, bias, cout)
    gain = send(gain, spread, (pieces, TILE, HALF))
    mixed = call(functools.partial(inverse_kernel, per, block), piece)(
        gain, spec, nyq, spare_gain, skip, received, t["inv"], t["twf"], t["ends"])
    mixed = exchange(mixed, ctx)
    return call(unpack_kernel, shape((seq_local, chan), bf16), halves)(mixed)


def solution(mesh):
    fine = Mesh(mesh.devices.reshape(2, -1, 2, 2, mesh.devices.shape[1] // 2),
                ("xh", "y", "core", "xl", "z"))
    ctx, ch = ("xh", "y", "core"), ("xl", "z")
    return jax.shard_map(
        on_device,
        mesh=fine,
        in_specs=(P(ctx, ch), P(ch, None), P(), P(None, ch), P(ch)),
        out_specs=P(ctx, ch),
        check_vma=False,
    )
```
